128 devices in a mesh: dp: 8 (over z, core), label: 16 (over x, y).
Axes of the slice: x: 4, y: 4, z: 4, core: 2. Of those that a mesh axis runs over, the one named last changes fastest.
Arguments:
- texts: bfloat16 [2048, 64, 768], P(('dp', 'label')), may hold values from -6 to 6
- lengths: int32 [2048], P(('dp', 'label')), may hold values from 8 to 64, as said below
- owners: int32 [2048, 1], P(('dp', 'label')), may hold values from 0 to 15; in each aligned block of 16 rows (0 to 15, 16 to 31, ...) at most 2 rows name the same one
- gain: float32 [768], replicated, may hold values from 0.1 to 1.9
- w_in: float32 [1536, 768], replicated, may hold values from -0.21875 to 0.21875
- w_out: float32 [1536, 768], replicated, may hold values from -0.15625 to 0.15625
- free_vectors: float32 [2048, 768], P(('dp', 'label')), may hold values from -0.21875 to 0.21875
- queries: float32 [4096, 768], P('dp'), may hold values from -6 to 6
- shortlist: int32 [4096, 4], P('dp'), may hold values from 0 to 15, all different within a row
- grad_scores: float32 [4096, 4096], P('dp', 'label'), may hold values from -6 to 6
Outputs:
- scores: float32 [4096, 4096], P('dp', 'label')
- free_grad: float32 [2048, 768], P(('dp', 'label'))
- w_in_grad: float32 [1536, 768], P(('dp', 'label'))
- w_out_grad: float32 [1536, 768], P(('dp', 'label'))
The draws below stay inside these ranges and needn't reach their ends.
Inputs may be any that keep to these rules, and one draw needn't show every extreme that they name: `lengths`: the 8 device blocks of texts that share one label index hold exactly 4608 tokens together. `owners`: among the labels of one device at most 2 share an owner, and in every draw some owner receives exactly 2 from some device. `shortlist`: each query names 4 different owners; every owner is named by some query.
All inputs are finite; a program needn't handle non-finite values.
Results may differ from the reference program's by a relative error of at most 0.0003.
Values may be sent and summed in bfloat16 or wider, within the bound.
No kernel may reach another device: no remote copies, remote signals or barrier semaphores. Data moves between devices by JAX's collectives and lax.ppermute only.
A program may use at most 128 MiB of HBM per device.

```python
import math
import jax
import jax.numpy as jnp
import numpy as np
from jax import lax

D = 768
FF = 1536
LMAX = 64
CAP = 2
SHORT = 4
TXT_DEV = 16
LABELS = 2048
QUERIES = 4096
OWN = 256
COLS = 4096
N_DP = 8
N_LABEL = 16


def draw_lengths(key, part):
    key = jax.random.fold_in(key, 11)
    lowest = LMAX // 8
    paired = LMAX + lowest
    halves = N_DP // 2
    drawn = jax.random.randint(key, (halves, N_LABEL, TXT_DEV), lowest, LMAX + 1)
    drawn = drawn.at[0, 0, 0].set(LMAX)
    longer = jnp.maximum(drawn, paired - drawn)
    shorter = paired - longer
    stacked = jnp.concatenate((longer, shorter), axis=0)
    order_keys = jax.random.split(jax.random.fold_in(key, 5), N_LABEL)
    orders = jax.vmap(lambda single: jax.random.permutation(single, N_DP))(order_keys)
    columns = jnp.arange(N_LABEL, dtype=jnp.int32)[None, :]
    placed = jnp.zeros((N_DP, N_LABEL, TXT_DEV), jnp.int32)
    placed = placed.at[orders.T, columns].set(stacked)
    return placed.reshape(N_DP * N_LABEL * TXT_DEV).astype(jnp.int32)


def levels(rng, extent, cuts, smallest, high):
    def one(axis_at, blocks):
        draws = jax.random.uniform(jax.random.fold_in(jax.random.fold_in(rng, 6), axis_at), (blocks,), jnp.float32, smallest / len(cuts), high / len(cuts))
        return jnp.repeat(jnp.exp(draws), extent[axis_at] // blocks).reshape((-1,) + (1,) * (len(extent) - axis_at - 1))

    loudness = one(*cuts[0])
    for cut in cuts[1:]:
        loudness = loudness * one(*cut)
    return loudness


def different_ones(stream_key, rows, number_of, top, lift):
    sequence = jax.random.permutation(jax.random.fold_in(stream_key, 1), number_of)
    pull = sequence
    for power in range(3):
        pull = pull * pull // number_of
    pull = pull * lift // number_of
    lots = jax.random.randint(jax.random.fold_in(stream_key, 2), (rows, number_of), 0, 4096) + pull
    sure = jax.random.permutation(jax.random.fold_in(stream_key, 3), rows)[jnp.arange(number_of) % rows]
    lots = jnp.where(jnp.arange(rows)[:, None] == sure[None, :], 1 << 14, lots)
    score = lots * number_of + jnp.arange(number_of)
    return lax.top_k(score.astype(jnp.int32), top)[1].astype(jnp.int32)


def deal_out(own_key, own, number, rows, number_of, top, limit, slope):
    ranking = jax.random.permutation(own_key, number_of)
    heavy_load, usual = portions_of(number_of, rows * top, limit, slope, True), portions_of(number_of, rows * top, limit, slope, False)
    places = jnp.arange(number_of)

    def named(sizes, rotation):
        used = int((sizes > 0).sum())
        fixed = max(1, used // 4)
        shifted = fixed + (places - fixed + rotation * (used - fixed)) % max(1, number_of - fixed)
        return jnp.zeros((number_of,), jnp.int32).at[ranking[jnp.where(places < fixed, places, shifted)]].set(jnp.asarray(sizes, jnp.int32))

    sizes = jnp.where(number % 4 == 0, named(heavy_load, number // 4), named(usual, number - number // 4 - 1))
    mixed = jax.random.permutation(jax.random.fold_in(own, 3), number_of)
    source_of, receiver = mixed[0:number_of // 2 * 2:2], mixed[1:number_of // 2 * 2:2]
    slack = jnp.minimum(sizes[source_of] - 1, limit - sizes[receiver]) // 2
    slack = jnp.where((source_of == ranking[0]) | (receiver == ranking[0]) | (sizes[receiver] == 0), 0, jnp.maximum(slack, 0))
    shifted = jax.random.randint(jax.random.fold_in(own, 4), (number_of // 2,), 0, 1 << 20) % (slack + 1)
    sizes = sizes.at[source_of].add(-shifted).at[receiver].add(shifted)
    labels = jnp.searchsorted(jnp.cumsum(sizes), jnp.arange(rows * top), side="right").astype(jnp.int32)
    listing = labels.reshape(top, rows).T
    listing = listing[jax.random.permutation(jax.random.fold_in(own, 1), rows)]
    rotation = jax.random.randint(jax.random.fold_in(own, 2), (rows, 1), 0, top)
    return jnp.take_along_axis(listing, (jnp.arange(top)[None, :] + rotation) % top, axis=1)


def portions_of(count, total, reach, skew, full):
    loads = [(1 << 20) // math.isqrt(standing ** skew) + 1 for standing in range(1, count + 1)]
    largest = reach if full else min(reach, max(-(-total // count), total * loads[0] // sum(loads)))
    least = 1 if total - largest >= count - 1 else 0
    given, surplus = [largest] + [least] * (count - 1), total - largest - least * (count - 1)
    while surplus > 0:
        movable = [i for i in range(1, count) if given[i] < largest] or [i for i in range(1, count) if given[i] < reach]
        whole, left = sum([loads[i] for i in movable]), surplus
        for i in movable:
            more = min(reach - given[i], max(1, left * loads[i] // whole), surplus)
            given[i] = given[i] + more
            surplus = surplus - more
    return np.array(given)


def bell_draw(key, extent, scale, limit, pieces=(), kind=jnp.bfloat16):
    entries = jax.random.normal(key, extent, jnp.float32) * scale
    if len(pieces) > 0:
        entries = levels(key, extent, pieces, -0.22, 0.18) * entries
    return jnp.clip(entries, min=-limit, max=limit).astype(kind)


def setup_inputs(seed: int = 0) -> dict:
    seeds = jax.random.split(jax.random.key(seed), 11)
    texts = bell_draw(seeds[0], (LABELS, LMAX, D), 1.0, 6.0, ((0, 128),))
    lengths = draw_lengths(jax.random.fold_in(seeds[10], 71), 0)
    owners_keys = jax.random.split(jax.random.fold_in(seeds[2], 1), LABELS // TXT_DEV)
    owners_turns = jax.random.permutation(jax.random.fold_in(seeds[2], 3), LABELS // TXT_DEV)
    owners = jax.vmap(lambda own, number: deal_out(jax.random.fold_in(seeds[2], 2), own, number, TXT_DEV, N_LABEL, 1, CAP, 2))(owners_keys, owners_turns).reshape((LABELS, 1))
    gain = jnp.clip(1.0 + 0.18 * jax.random.normal(seeds[3], (D,), jnp.float32), 0.1, 1.9)
    w_in = bell_draw(seeds[4], (FF, D), D ** -0.5, 0.21875, (), jnp.float32)
    w_out = bell_draw(seeds[5], (FF, D), FF ** -0.5, 0.15625, (), jnp.float32)
    free_vectors = bell_draw(seeds[6], (LABELS, D), D ** -0.5, 0.21875, ((0, 128),), jnp.float32)
    queries = bell_draw(seeds[7], (QUERIES, D), 1.0, 6.0, ((0, 8),), jnp.float32)
    shortlist = different_ones(seeds[8], QUERIES, N_LABEL, SHORT, 2048)
    grad_scores = bell_draw(seeds[9], (QUERIES, COLS), 1.0, 6.0, ((0, 8), (1, 16)), jnp.float32)
    return dict(texts=texts, lengths=lengths, owners=owners, gain=gain, w_in=w_in, w_out=w_out, free_vectors=free_vectors, queries=queries, shortlist=shortlist, grad_scores=grad_scores)


highest = lax.Precision.HIGHEST

def pool(hidden, lengths):
    positions = jnp.arange(hidden.shape[1], dtype=jnp.int32)
    weights = (positions[None, :] < lengths[:, None]).astype(jnp.float32) / lengths[:, None].astype(jnp.float32)
    pooled = jnp.einsum('lt,ltd->ld', weights, hidden, precision=highest)
    return pooled * lax.rsqrt(lax.optimization_barrier(jnp.sum(pooled * pooled, axis=-1, keepdims=True)) + 1e-06)

def encode_block(texts, lengths, gain, w_in, w_out):
    inputs = texts.astype(jnp.float32)
    inv_scale = lax.rsqrt(lax.optimization_barrier(jnp.mean(inputs * inputs, axis=-1, keepdims=True)) + 1e-05)
    normed = inputs * inv_scale * gain
    pre_act = jnp.einsum('ltd,fd->ltf', normed, w_in, precision=highest)
    hidden = inputs + jnp.einsum('ltf,fd->ltd', jax.nn.gelu(pre_act), w_out, precision=highest)
    return pool(hidden, lengths)

def slot_columns(owner):
    label_count = owner.shape[0]
    one_hot = (owner[:, None] == jnp.arange(N_LABEL, dtype=jnp.int32)[None, :]).astype(jnp.int32)
    blocks = one_hot.reshape(label_count // TXT_DEV, TXT_DEV, N_LABEL)
    before = jnp.cumsum(blocks, axis=1) - blocks
    slot_rank = lax.optimization_barrier(jnp.sum(before * blocks, axis=-1)).reshape(label_count)
    device = jnp.arange(label_count, dtype=jnp.int32) // TXT_DEV
    return (owner * OWN + device * CAP + slot_rank).astype(jnp.int32)

def reference(texts, lengths, owners, gain, w_in, w_out, free_vectors, queries, shortlist, grad_scores):
    block_count = LABELS // TXT_DEV
    text_blocks = texts.reshape(block_count, TXT_DEV, LMAX, D)
    length_blocks = lengths.reshape(block_count, TXT_DEV)

    def embed_one(packed):
        return encode_block(packed[0], packed[1], gain, w_in, w_out)
    embeds = lax.map(embed_one, (text_blocks, length_blocks)).reshape(LABELS, D)
    label_sums = embeds + free_vectors
    columns = slot_columns(owners[:, 0])
    table = jnp.zeros((COLS, D), jnp.float32).at[columns].set(label_sums)
    picked = jnp.any(shortlist[:, :, None] == jnp.arange(N_LABEL, dtype=jnp.int32)[None, None, :], axis=1)
    keep = jnp.repeat(picked.astype(jnp.float32), OWN, axis=1)
    scores = jnp.dot(queries, table.T, precision=highest) * keep
    table_grad = jnp.dot((grad_scores * keep).T, queries, precision=highest)
    free_grad = table_grad[columns]

    def accumulate(carry, packed):
        block_texts, block_lengths, block_grad = packed
        _, pull_back = jax.vjp(lambda first, second: encode_block(block_texts, block_lengths, gain, first, second), w_in, w_out)
        first_grad, second_grad = pull_back(block_grad)
        return ((carry[0] + first_grad, carry[1] + second_grad), None)
    zeros = jnp.zeros((FF, D), jnp.float32)
    grads, _ = lax.scan(accumulate, (zeros, zeros), (text_blocks, length_blocks, free_grad.reshape(block_count, TXT_DEV, D)))
    return (scores, free_grad, grads[0], grads[1])
```

```python
import math

import jax
import jax.numpy as jnp
from jax import lax
from jax.experimental import pallas as pl
from jax.experimental.pallas import tpu as pltpu
from jax.sharding import Mesh, PartitionSpec as P

N_Z, N_CORE, N_X, N_Y = 4, 2, 4, 4
N_LABEL = N_X * N_Y
TXT = 16
LMAX = 64
D = 768
FF = 1536
HALF = FF // 2
BLOCK = FF // (N_Z * N_CORE)
ROWS = BLOCK // N_LABEL
CAP = 2
SLOTS = N_LABEL * CAP
QROWS = 512
TOKENS = 256
TEXTS_STEP = TOKENS // LMAX
STEPS = 2 * TXT // TEXTS_STEP
C0 = math.sqrt(2.0 / math.pi)
C1 = C0 * 0.044715
MIB = 1024 * 1024

f32 = jnp.float32
bf16 = jnp.bfloat16
N_CHIPS = N_Z * N_LABEL
CHIP_SLOTS = N_CHIPS * CAP
PIECES = D // 128
CHUNK = PIECES * ROWS
SLOT_ROWS = CAP * PIECES
AT_W_OUT = N_Z * CHUNK
AT_POWERS = AT_W_OUT + CHUNK
AT_LABELS = AT_POWERS + 16
SENT_ROWS = AT_LABELS + 2 * SLOT_ROWS
MOVED_ROWS = CHUNK + N_LABEL * SLOT_ROWS
LABEL_SCALE = 256.0
PARTS = 4
PART = 2 * TXT * LMAX // PARTS
LABEL = ("x", "y")


def split(value):
    high = value.astype(bf16)
    return high, (value - high.astype(f32)).astype(bf16)


def dot(a, b, dims):
    return lax.dot_general(a, b, (dims, ((), ())), preferred_element_type=f32)


def dot3(a, b, dims):
    a_high, a_low = split(a)
    b_high, b_low = split(b)
    return dot(a_high, b_high, dims) + (dot(a_high, b_low, dims) + dot(a_low, b_high, dims))


def params(mib):
    return pltpu.CompilerParams(vmem_limit_bytes=mib * MIB)


def vmem(count):
    return [pl.BlockSpec(memory_space=pltpu.VMEM)] * count


def smem(count):
    return [pl.BlockSpec(memory_space=pltpu.SMEM)] * count


def is_kept(shortlist_ref, label):
    row = jnp.max((shortlist_ref[...] == label).astype(f32), axis=0, keepdims=True)
    return jnp.broadcast_to(row, (8, QROWS)).T[:, :1]


def iota(shape, axis):
    return lax.broadcasted_iota(jnp.int32, shape, axis)


def in_hbm(value):
    return pltpu.with_memory_space_constraint(value, pltpu.HBM)


def cost(flops, nbytes):
    return pl.CostEstimate(flops=flops, bytes_accessed=nbytes, transcendentals=0)


ANY = pl.BlockSpec(memory_space=pl.ANY)
HBM = pl.BlockSpec(memory_space=pltpu.HBM)
NN, NT, TN = ((1,), (0,)), ((1,), (1,)), ((0,), (0,))


def partial_kernel(place_ref, shortlist_ref, grad_ref, queries_ref, own_ref, other_ref):
    weighted = grad_ref[...] * is_kept(shortlist_ref, place_ref[1])
    size = 2 * CHIP_SLOTS
    target = iota((size, size), 1)
    half = target // CHIP_SLOTS
    rank = target // N_CHIPS % CAP
    z = target // N_LABEL % N_Z
    lab = target % N_LABEL
    flip = jnp.where(half == 0, place_ref[0], 1 - place_ref[0])
    source = ((z * N_CORE + flip) * N_LABEL + lab) * CAP + rank
    order = (iota((size, size), 0) == source).astype(bf16)
    w_high, w_low = (dot(part, order, NN).astype(bf16) for part in split(weighted))
    q_high, q_low = split(queries_ref[...])
    total = dot(w_high, q_high, TN) + (dot(w_high, q_low, TN) + dot(w_low, q_high, TN))
    for h, ref in enumerate((own_ref, other_ref)):
        for r in range(CAP):
            start = h * CHIP_SLOTS + r * N_CHIPS
            for j in range(PIECES):
                ref[pl.ds(PIECES * r + j, N_CHIPS, stride=16)] = total[start : start + N_CHIPS, j * 128 : (j + 1) * 128]


def slot_partials(place, shortlist, grad_scores, queries):
    shape = jax.ShapeDtypeStruct((N_CHIPS * 16, 128), f32)
    return pl.pallas_call(
        partial_kernel,
        out_shape=(shape, shape),
        in_specs=smem(1) + vmem(3),
        out_specs=tuple(vmem(2)),
        compiler_params=params(24),
        cost_estimate=cost(6 * QROWS * 256 * D, 4 * 10**6),
        name="slot_partials",
    )(place, shortlist, grad_scores, queries)


def forward_kernel(
    place_ref,
    lengths_ref,
    gain_ref,
    own_ref,
    other_ref,
    w_in_ref,
    w_out_ref,
    slope_ref,
    pooled_ref,
    sums_ref,
    out_high_ref,
    out_low_ref,
    w_in_buf,
    w_out_buf,
    x_buf,
    slope_buf,
    w_high,
    w_low,
    pooled,
    pooled_x,
    w_sem,
    x_sem,
    slope_sem,
):
    core = place_ref[0]
    w_copies = [
        pltpu.make_async_copy(ref.at[:, core], buf, w_sem.at[i])
        for i, (ref, buf) in enumerate(((w_in_ref, w_in_buf), (w_out_ref, w_out_buf)))
    ]
    x_copies = [pltpu.make_async_copy(ref, x_buf.at[i], x_sem.at[i]) for i, ref in enumerate((own_ref, other_ref))]
    w_copies[0].start()
    x_copies[0].start()
    x_copies[1].start()
    w_copies[1].start()
    w_copies[0].wait()
    for z in range(N_Z):
        rows = slice(z * BLOCK, (z + 1) * BLOCK)
        w_high[rows], w_low[rows] = split(w_in_buf[z] * gain_ref[...])
    position = iota((LMAX, 1), 0)

    def store(step):
        slot = lax.rem(step, 2)
        rows = pl.ds(pl.multiple_of(step * TOKENS, TOKENS), TOKENS)
        return pltpu.make_async_copy(slope_buf.at[slot], slope_ref.at[rows], slope_sem.at[slot])

    def run(which):
        def body(s, _):
            x = x_buf[which, pl.ds(pl.multiple_of(s * TOKENS, TOKENS), TOKENS)]
            xf = x.astype(f32)
            inverse = lax.rsqrt(jnp.sum(xf * xf, axis=1, keepdims=True) * (1.0 / D) + 1e-05)
            step = which * (STEPS // 2) + s
            slot = lax.rem(step, 2)

            @pl.when(step >= 2)
            def _():
                store(step - 2).wait()

            weights = []
            for i in range(TEXTS_STEP):
                length = lengths_ref[step * TEXTS_STEP + i]
                scale = 1.0 / jnp.full((1, 1), length, jnp.int32).astype(f32)
                weights.append(jnp.where(position < length, scale, 0.0))
                rows = slice(i * LMAX, (i + 1) * LMAX)
                pooled_x[step, i : i + 1] = jnp.sum(xf[rows] * weights[i], axis=0, keepdims=True)
            weight = jnp.concatenate(weights, axis=0)
            scaled = weight * inverse
            for j in range(HALF // 256):
                cols = slice(j * 256, (j + 1) * 256)
                p = (dot(x, w_high[cols], NT) + dot(x, w_low[cols], NT)) * inverse
                p2 = p * p
                half = 0.5 + 0.5 * jnp.tanh(p * (C0 + C1 * p2))
                act = p * half
                slope = half + (act - act * half) * (2.0 * C0 + 6.0 * C1 * p2)
                slope_buf[slot, :, cols] = slope * scaled
                act = act * weight
                for i in range(TEXTS_STEP):
                    rows = slice(i * LMAX, (i + 1) * LMAX)
                    pooled[step, i : i + 1, cols] = jnp.sum(act[rows], axis=0, keepdims=True)
            store(step).start()
            return 0

        x_copies[which].wait()
        lax.fori_loop(0, STEPS // 2, body, 0)

    run(0)
    run(1)
    w_copies[1].wait()
    acts = jnp.concatenate([pooled[i] for i in range(STEPS)], axis=0)
    total = 0.5 * jnp.concatenate([pooled_x[i] for i in range(STEPS)], axis=0)
    for z in range(N_Z):
        high, low = split(w_out_buf[z])
        out_high_ref[z] = high
        out_low_ref[z] = low
        a = acts[:, z * BLOCK : (z + 1) * BLOCK]
        pooled_ref[z] = jnp.concatenate([a, jnp.zeros((2 * TXT, 256 - BLOCK), f32)], axis=1)
        a_high, a_low = split(a)
        total = total + (dot(a_high, high, NN) + (dot(a_high, low, NN) + dot(a_low, high, NN)))
    sums_ref[...] = total
    for step in (STEPS - 2, STEPS - 1):
        store(step).wait()


def forward(place, lengths, gain, own, other, w_in, w_out):
    tokens = 2 * TXT * LMAX
    shape = jax.ShapeDtypeStruct
    return pl.pallas_call(
        forward_kernel,
        out_shape=(
            pltpu.HBM((tokens, HALF), f32),
            shape((N_Z, 2 * TXT, 256), f32),
            shape((2 * TXT, D), f32),
            shape((N_Z, BLOCK, D), bf16),
            shape((N_Z, BLOCK, D), bf16),
        ),
        in_specs=smem(2) + vmem(1) + [HBM, ANY, HBM, HBM],
        out_specs=(HBM, *vmem(4)),
        scratch_shapes=[
            pltpu.VMEM((N_Z, BLOCK, D), f32),
            pltpu.VMEM((N_Z, BLOCK, D), f32),
            pltpu.VMEM((2, TXT * LMAX, D), bf16),
            pltpu.VMEM((2, TOKENS, HALF), f32),
            pltpu.VMEM((HALF, D), bf16),
            pltpu.VMEM((HALF, D), bf16),
            pltpu.VMEM((STEPS, TEXTS_STEP, HALF), f32),
            pltpu.VMEM((STEPS, TEXTS_STEP, D), f32),
            pltpu.SemaphoreType.DMA((2,)),
            pltpu.SemaphoreType.DMA((2,)),
            pltpu.SemaphoreType.DMA((2,)),
        ],
        compiler_params=params(24),
        cost_estimate=cost(10 * tokens * HALF * D, 8 * 10**6),
        name="encoder_forward",
    )(place, lengths, gain, in_hbm(own), other, in_hbm(w_in), in_hbm(w_out))


def unit_rows(sums):
    return lax.rsqrt(jnp.sum(sums * sums, axis=-1, keepdims=True) + 1e-06)


def each_label(owners_ref, counts, put):
    for o in range(N_LABEL):
        counts[o] = 0
    for i in range(TXT):
        owner = owners_ref[i]
        rank = counts[owner]
        counts[owner] = rank + 1
        put(i, owner, jnp.minimum(rank, CAP - 1))


def label_kernel(owners_ref, part_ref, came_ref, free_ref, sums_ref, out_ref, counts):
    own = part_ref[:TXT] + came_ref[TXT:]
    sums_ref[:TXT] = own
    sums_ref[TXT:] = part_ref[TXT:] + came_ref[:TXT]
    scaled = (own * unit_rows(own) + free_ref[...]) * LABEL_SCALE
    high = scaled.astype(bf16).astype(f32)
    low = scaled - high
    out_ref[...] = jnp.zeros_like(out_ref)

    def put(i, owner, rank):
        for k, value in enumerate((high, low)):
            for j in range(PIECES):
                row = pl.ds((k * CAP + rank) * PIECES + j, 1)
                out_ref[owner, row] = value[i : i + 1, j * 128 : (j + 1) * 128]

    each_label(owners_ref, counts, put)


def labels(owners, part, came, free_vectors):
    return pl.pallas_call(
        label_kernel,
        out_shape=(
            jax.ShapeDtypeStruct((2 * TXT, D), f32),
            jax.ShapeDtypeStruct((N_LABEL, 2 * SLOT_ROWS, 128), f32),
        ),
        in_specs=smem(1) + vmem(3),
        out_specs=tuple(vmem(2)),
        scratch_shapes=[pltpu.SMEM((N_LABEL,), jnp.int32)],
        compiler_params=params(8),
        cost_estimate=cost(10**6, 8 * 10**5),
        name="label_vectors",
    )(owners, part, came, free_vectors)


def scores_kernel(place_ref, shortlist_ref, queries_ref, own_ref, other_ref, out_ref):
    size = 2 * CHIP_SLOTS
    column = iota((size, size), 0)
    rank = column % CAP
    lab = column // CAP % N_LABEL
    core = column // (CAP * N_LABEL) % N_CORE
    z = column // (CAP * N_LABEL * N_CORE)
    half = jnp.where(core == place_ref[0], 0, 1)
    source = half * CHIP_SLOTS + rank * N_CHIPS + z * N_LABEL + lab
    order = (iota((size, size), 1) == source).astype(bf16)
    table = jnp.concatenate(
        [
            jnp.concatenate(
                [ref[pl.ds(PIECES * r + j, N_CHIPS, stride=SLOT_ROWS)] for j in range(PIECES)],
                axis=1,
            )
            for ref in (own_ref, other_ref)
            for r in range(CAP)
        ],
        axis=0,
    )
    t_high, t_low = (dot(order, part, NN).astype(bf16) for part in split(table))
    q_high, q_low = split(queries_ref[...])
    scores = dot(q_high, t_high, NT) + (dot(q_high, t_low, NT) + dot(q_low, t_high, NT))
    out_ref[...] = scores * is_kept(shortlist_ref, place_ref[1])


def slot_scores(place, shortlist, queries, own, other):
    return pl.pallas_call(
        scores_kernel,
        out_shape=jax.ShapeDtypeStruct((QROWS, 2 * CHIP_SLOTS), f32),
        in_specs=smem(1) + vmem(4),
        out_specs=pl.BlockSpec(memory_space=pltpu.VMEM),
        compiler_params=params(24),
        cost_estimate=cost(6 * QROWS * 256 * D, 4 * 10**6),
        name="slot_scores",
    )(place, shortlist, queries, own, other)


def return_kernel(owners_ref, came_ref, out_ref, counts):
    def put(i, owner, rank):
        value = came_ref[owner]
        for z in range(1, N_Z):
            value = value + came_ref[z * N_LABEL + owner]
        value = jnp.where(rank == 0, value[:PIECES], value[PIECES : 2 * PIECES])
        for j in range(PIECES):
            out_ref[i : i + 1, j * 128 : (j + 1) * 128] = value[j : j + 1]

    each_label(owners_ref, counts, put)


def returned(owners, came):
    return pl.pallas_call(
        return_kernel,
        out_shape=jax.ShapeDtypeStruct((TXT, D), f32),
        in_specs=smem(1) + vmem(1),
        out_specs=pl.BlockSpec(memory_space=pltpu.VMEM),
        scratch_shapes=[pltpu.SMEM((N_LABEL,), jnp.int32)],
        compiler_params=params(8),
        cost_estimate=cost(10**5, 5 * 10**5),
        name="returned_gradients",
    )(owners, came)


def pull_kernel(place_ref, free_own_ref, free_other_ref, sums_ref, high_ref, low_ref, pooled_ref, back_ref, *outs):
    free = jnp.concatenate([free_own_ref[...], free_other_ref[...]], axis=0)
    sums = sums_ref[...]
    unit = unit_rows(sums)
    along = jnp.sum(sums * free, axis=-1, keepdims=True)
    pulled = unit * free - (unit * unit * unit * along) * sums
    p_high, p_low = split(pulled)
    back_ref[...] = jnp.concatenate(
        [
            dot(p_high, high_ref[z], NT) + (dot(p_high, low_ref[z], NT) + dot(p_low, high_ref[z], NT))
            for z in range(N_Z)
        ],
        axis=1,
    )
    for f in range(N_Z):
        outs[f][:, :256] = pooled_ref[lax.rem(place_ref[4] + f, N_Z)]
        outs[f][:, 256:] = pulled


def pull(place, free_own, free_other, sums, high, low, pooled):
    return pl.pallas_call(
        pull_kernel,
        out_shape=(jax.ShapeDtypeStruct((2 * TXT, HALF), f32),)
        + (jax.ShapeDtypeStruct((2 * TXT, 256 + D), f32),) * N_Z,
        in_specs=smem(1) + vmem(6),
        out_specs=tuple(vmem(1 + N_Z)),
        compiler_params=params(12),
        cost_estimate=cost(6 * 32 * HALF * D, 3 * 10**6),
        name="pull_back",
    )(place, free_own, free_other, sums, high, low, pooled)


def backward_kernel(back_ref, gain_ref, own_ref, other_ref, slope_ref, grad, largest, x_buf, slope_buf, sem):
    copies = []
    for q in range(PARTS):
        x_rows = slice(q % (PARTS // 2) * PART, (q % (PARTS // 2) + 1) * PART)
        x_ref = (own_ref, other_ref)[q // (PARTS // 2)]
        rows = slice(q * PART, (q + 1) * PART)
        copies.append(
            (
                pltpu.make_async_copy(x_ref.at[x_rows], x_buf.at[q], sem.at[0, q]),
                pltpu.make_async_copy(slope_ref.at[rows], slope_buf.at[q], sem.at[1, q]),
            )
        )
    for pair in copies:
        for copy in pair:
            copy.start()
    for q in range(PARTS):
        for copy in copies[q]:
            copy.wait()

        def product(j, _):
            cols = pl.ds(pl.multiple_of(j * 256, 256), 256)
            total = jnp.zeros((256, D), f32)
            for i in range(PART // TOKENS):
                pieces = []
                for t in range(i * TEXTS_STEP, (i + 1) * TEXTS_STEP):
                    text = q * (PART // LMAX) + t
                    pieces.append(slope_buf[q, t * LMAX : (t + 1) * LMAX, cols] * back_ref[text : text + 1, cols])
                high, low = split(jnp.concatenate(pieces, axis=0))
                x = x_buf[q, i * TOKENS : (i + 1) * TOKENS]
                total = total + (dot(high, x, TN) + dot(low, x, TN))
            if q > 0:
                total = total + grad[cols]
            if q == PARTS - 1:
                total = total * gain_ref[...]
                largest[pl.ds(j, 1)] = jnp.max(jnp.abs(total), axis=0, keepdims=True)
            grad[cols] = total
            return 0

        lax.fori_loop(0, HALF // 256, product, 0)


def backward(back, gain, own, other, slope):
    tokens = 2 * TXT * LMAX
    shape = jax.ShapeDtypeStruct
    return pl.pallas_call(
        backward_kernel,
        out_shape=(shape((HALF, D), f32), shape((HALF // 256, D), f32)),
        in_specs=vmem(2) + [HBM, ANY, HBM],
        out_specs=tuple(vmem(2)),
        scratch_shapes=[
            pltpu.VMEM((PARTS, PART, D), bf16),
            pltpu.VMEM((PARTS, PART, HALF), f32),
            pltpu.SemaphoreType.DMA((2, PARTS)),
        ],
        compiler_params=params(24),
        cost_estimate=cost(5 * tokens * HALF * D, 4 * 10**6),
        name="encoder_backward",
    )(back, gain, in_hbm(own), other, in_hbm(slope))


def power_of(top):
    return jnp.clip(jnp.floor(14.0 - jnp.log2(jnp.maximum(top, 1e-30))), -100.0, 100.0)


def finish_kernel(grad_ref, largest_ref, labels_ref, *rest):
    factors, out_ref = rest[:N_Z], rest[N_Z]
    acts = jnp.concatenate([ref[:, :BLOCK] for ref in factors], axis=0)
    pulled = jnp.concatenate([ref[:, 256:] for ref in factors], axis=0)
    block = dot3(acts, pulled, TN)
    top = jnp.max(jnp.max(largest_ref[...], axis=0, keepdims=True), axis=1, keepdims=True)
    block_top = jnp.max(jnp.max(jnp.abs(block), axis=0, keepdims=True), axis=1, keepdims=True)
    power, block_power = power_of(top), power_of(block_top)
    scale = jnp.exp2(power)
    block = block * jnp.exp2(block_power)
    powers = jnp.concatenate([jnp.broadcast_to(power, (8, 128)), jnp.broadcast_to(block_power, (8, 128))], axis=0)
    for lab in range(N_LABEL):
        for j in range(PIECES):
            start = AT_W_OUT + j * ROWS
            out_ref[lab, start : start + ROWS] = block[lab * ROWS : (lab + 1) * ROWS, j * 128 : (j + 1) * 128]
        out_ref[lab, AT_POWERS:AT_LABELS] = powers
        out_ref[lab, AT_LABELS:] = labels_ref[lab]
    for z in range(N_Z):

        def place_rows(k, _):
            start = z * BLOCK + k * 2 * ROWS
            rows = grad_ref[pl.ds(pl.multiple_of(start, 2 * ROWS), 2 * ROWS)] * scale
            for g in range(2):
                for j in range(PIECES):
                    piece = rows[g * ROWS : (g + 1) * ROWS, j * 128 : (j + 1) * 128]
                    first = z * CHUNK + j * ROWS
                    out_ref[2 * k + g, first : first + ROWS] = piece
            return 0

        lax.fori_loop(0, N_LABEL // 2, place_rows, 0)


def finish(grad, largest, label_rows, factors):
    return pl.pallas_call(
        finish_kernel,
        out_shape=jax.ShapeDtypeStruct((N_LABEL, SENT_ROWS, 128), f32),
        in_specs=vmem(3 + N_Z),
        out_specs=pl.BlockSpec(memory_space=pltpu.VMEM),
        compiler_params=params(16),
        cost_estimate=cost(10**9, 5 * 10**6),
        name="finish_gradients",
    )(grad, largest, label_rows, *factors)


def unpieced(rows):
    return jnp.concatenate([rows[j * ROWS : (j + 1) * ROWS] for j in range(PIECES)], axis=1)


def middle_kernel(place_ref, came_ref, w_out_ref, *outs):
    total = jnp.zeros((AT_W_OUT, 128), f32)
    block = jnp.zeros((CHUNK, 128), f32)
    vectors = []
    for lab in range(N_LABEL):
        total = total + came_ref[lab, :AT_W_OUT] * jnp.exp2(-came_ref[lab, AT_POWERS : AT_POWERS + 1])
        block = block + came_ref[lab, AT_W_OUT:AT_POWERS] * jnp.exp2(-came_ref[lab, AT_POWERS + 8 : AT_POWERS + 9])
        high = came_ref[lab, AT_LABELS : AT_LABELS + SLOT_ROWS]
        low = came_ref[lab, AT_LABELS + SLOT_ROWS :]
        vectors.append((high + low) * (1.0 / LABEL_SCALE))
    w_out_ref[...] = unpieced(block)
    vectors = jnp.concatenate(vectors, axis=0)
    for f in range(N_Z):
        outs[f][CHUNK:] = vectors
    for z in range(N_Z):
        for f in range(N_Z):

            @pl.when(lax.rem(place_ref[4] + f, N_Z) == z)
            def _(z=z, f=f):
                outs[f][:CHUNK] = total[z * CHUNK : (z + 1) * CHUNK]


def middle(place, came):
    return pl.pallas_call(
        middle_kernel,
        out_shape=(jax.ShapeDtypeStruct((ROWS, D), f32),)
        + (jax.ShapeDtypeStruct((MOVED_ROWS, 128), f32),) * N_Z,
        in_specs=smem(1) + vmem(1),
        out_specs=tuple(vmem(1 + N_Z)),
        compiler_params=params(16),
        cost_estimate=cost(10**7, 4 * 10**6),
        name="plane_sums",
    )(place, came)


def last_kernel(place_ref, *rest):
    blocks, (w_in_ref, table_ref) = rest[:N_Z], rest[N_Z:]
    total = blocks[0][:CHUNK]
    for f in range(1, N_Z):
        total = total + blocks[f][:CHUNK]
    w_in_ref[...] = unpieced(total)
    size = N_LABEL * SLOT_ROWS
    for f in range(N_Z):
        z = lax.rem(place_ref[4] - f + N_Z, N_Z)
        table_ref[pl.ds(pl.multiple_of(z * size, size), size)] = blocks[f][CHUNK:]


def last(place, blocks):
    return pl.pallas_call(
        last_kernel,
        out_shape=(
            jax.ShapeDtypeStruct((ROWS, D), f32),
            jax.ShapeDtypeStruct((N_CHIPS * SLOT_ROWS, 128), f32),
        ),
        in_specs=smem(1) + vmem(N_Z),
        out_specs=tuple(vmem(2)),
        compiler_params=params(8),
        cost_estimate=cost(10**6, 10**6),
        name="z_sums",
    )(place, *blocks)


def swap(value):
    return lax.ppermute(value, "core", ((0, 1), (1, 0)))


def shift(blocks, axis):
    moved = [lax.ppermute(blocks[k], axis, [(i, (i + k) % 4) for i in range(4)]) for k in range(1, 4)]
    return [blocks[0]] + moved


def exchange(value, axes):
    return lax.all_to_all(value, axes, split_axis=0, concat_axis=0, tiled=True)


def local(texts, lengths, owners, gain, w_in, w_out, free_vectors, queries, shortlist, grad_scores):
    core, x, y, z = (lax.axis_index(name) for name in ("core", "x", "y", "z"))
    place = jnp.stack([core, x * N_Y + y, x, y, z]).astype(jnp.int32)
    own = texts.reshape(TXT * LMAX, D)
    other = swap(own)
    both_lengths = jnp.concatenate([lengths, swap(lengths)])
    owner_ids = owners[:, 0]
    names = shortlist.T
    gain_row = gain.reshape(1, D)
    w_in_blocks = w_in.reshape(N_Z, N_CORE, BLOCK, D)
    w_out_blocks = w_out.reshape(N_Z, N_CORE, BLOCK, D)

    kept, sent = slot_partials(place, names, grad_scores, queries)
    slots = exchange((kept + swap(sent)).reshape(N_CHIPS, 16, 128), ("z", "x", "y"))

    slope, pooled, part, high, low = forward(place, both_lengths, gain_row, own, other, w_in_blocks, w_out_blocks)
    sums, label_rows = labels(owner_ids, part, swap(part), free_vectors)

    free_grad = returned(owner_ids, slots)
    back, *factors = pull(place, free_grad, swap(free_grad), sums, high, low, pooled)
    factors = shift(factors, "z")
    grad, largest = backward(back, gain_row, own, other, slope)
    sent_rows = finish(grad, largest, label_rows, factors)
    came = exchange(sent_rows.astype(jnp.float16), LABEL).astype(f32)
    w_out_grad, *moved = middle(place, came)
    w_in_grad, table = last(place, shift(moved, "z"))
    scores = slot_scores(place, names, queries, table, swap(table))
    return scores, free_grad, w_in_grad, w_out_grad


def solution(mesh):
    fine = Mesh(mesh.devices.reshape(N_Z, N_CORE, N_X, N_Y), ("z", "core", "x", "y"))
    dp, every = ("z", "core"), ("z", "core", "x", "y")
    placed = (
        P(every, None, None),
        P(every),
        P(every, None),
        P(),
        P(),
        P(),
        P(every, None),
        P(dp, None),
        P(dp, None),
        P(dp, LABEL),
    )
    return jax.shard_map(
        local,
        mesh=fine,
        in_specs=placed,
        out_specs=(
            P(dp, LABEL),
            P(every, None),
            P(every, None),
            P(every, None),
        ),
        check_vma=False,
    )
```

```python
import functools
import math

import jax
import jax.numpy as jnp
from jax import lax
from jax.experimental import pallas as pl
from jax.experimental.pallas import tpu as pltpu
from jax.sharding import Mesh, PartitionSpec as P

N_Z, N_CORE, N_X, N_Y = 4, 2, 4, 4
N_LABEL = N_X * N_Y
TXT = 16
LMAX = 64
D = 768
FF = 1536
HALF = FF // 2
BLOCK = FF // (N_Z * N_CORE)
ROWS = BLOCK // N_LABEL
CAP = 2
SLOTS = N_LABEL * CAP
QROWS = 512
TOKENS = 256
TEXTS_STEP = TOKENS // LMAX
STEPS = 2 * TXT // TEXTS_STEP
C0 = math.sqrt(2.0 / math.pi)
C1 = C0 * 0.044715
MIB = 1024 * 1024

f32 = jnp.float32
bf16 = jnp.bfloat16
N_CHIPS = N_Z * N_LABEL
CHIP_SLOTS = N_CHIPS * CAP
PIECES = D // 128
CHUNK = PIECES * ROWS
SLOT_ROWS = CAP * PIECES
AT_W_OUT = N_Z * CHUNK
AT_POWERS = AT_W_OUT + CHUNK
AT_LABELS = AT_POWERS + 8
SENT_ROWS = AT_LABELS + N_Z * SLOT_ROWS
FACTOR_ROWS = 2 * TXT * (256 + D) // 128
MOVED_ROWS = FACTOR_ROWS + N_LABEL * SLOT_ROWS
LABEL_SCALE = 256.0
PARTS = 2
PART = 2 * TXT * LMAX // PARTS
LABEL = ("x", "y")


def split(value):
    high = value.astype(bf16)
    return high, (value - high.astype(f32)).astype(bf16)


def dot(a, b, dims):
    return lax.dot_general(a, b, (dims, ((), ())), preferred_element_type=f32)


def dot3(a, b, dims):
    a_high, a_low = split(a)
    b_high, b_low = split(b)
    return dot(a_high, b_high, dims) + (dot(a_high, b_low, dims) + dot(a_low, b_high, dims))


def params(mib):
    return pltpu.CompilerParams(vmem_limit_bytes=mib * MIB)


def vmem(count):
    return [pl.BlockSpec(memory_space=pltpu.VMEM)] * count


def smem(count):
    return [pl.BlockSpec(memory_space=pltpu.SMEM)] * count


def is_kept(shortlist_ref, label):
    row = jnp.max((shortlist_ref[...] == label).astype(f32), axis=0, keepdims=True)
    return jnp.broadcast_to(row, (8, QROWS)).T[:, :1]


def iota(shape, axis):
    return lax.broadcasted_iota(jnp.int32, shape, axis)


def in_hbm(value):
    return pltpu.with_memory_space_constraint(value, pltpu.HBM)


def cost(flops, nbytes):
    return pl.CostEstimate(flops=flops, bytes_accessed=nbytes, transcendentals=0)


ANY = pl.BlockSpec(memory_space=pl.ANY)
HBM = pl.BlockSpec(memory_space=pltpu.HBM)
NN, NT, TN = ((1,), (0,)), ((1,), (1,)), ((0,), (0,))


def partial_kernel(place_ref, shortlist_ref, grad_ref, queries_ref, own_ref, other_ref):
    weighted = grad_ref[...] * is_kept(shortlist_ref, place_ref[1])
    size = 2 * CHIP_SLOTS
    target = iota((size, size), 1)
    half = target // CHIP_SLOTS
    rank = target // N_CHIPS % CAP
    z = target // N_LABEL % N_Z
    lab = target % N_LABEL
    flip = jnp.where(half == 0, place_ref[0], 1 - place_ref[0])
    source = ((z * N_CORE + flip) * N_LABEL + lab) * CAP + rank
    order = (iota((size, size), 0) == source).astype(bf16)
    w_high, w_low = (dot(part, order, NN).astype(bf16) for part in split(weighted))
    q_high, q_low = split(queries_ref[...])
    total = dot(w_high, q_high, TN) + (dot(w_high, q_low, TN) + dot(w_low, q_high, TN))
    for h, ref in enumerate((own_ref, other_ref)):
        for r in range(CAP):
            start = h * CHIP_SLOTS + r * N_CHIPS
            for j in range(PIECES):
                ref[pl.ds(PIECES * r + j, N_CHIPS, stride=16)] = total[start : start + N_CHIPS, j * 128 : (j + 1) * 128]


def slot_partials(place, shortlist, grad_scores, queries):
    shape = jax.ShapeDtypeStruct((N_CHIPS * 16, 128), f32)
    return pl.pallas_call(
        partial_kernel,
        out_shape=(shape, shape),
        in_specs=smem(1) + vmem(3),
        out_specs=tuple(vmem(2)),
        compiler_params=params(24),
        cost_estimate=cost(6 * QROWS * 256 * D, 4 * 10**6),
        name="slot_partials",
    )(place, in_hbm(shortlist), in_hbm(grad_scores), in_hbm(queries))


def forward_kernel(
    place_ref,
    lengths_ref,
    gain_ref,
    own_ref,
    other_ref,
    w_in_ref,
    w_out_ref,
    slope_ref,
    pooled_ref,
    sums_ref,
    out_high_ref,
    out_low_ref,
    w_in_buf,
    w_out_buf,
    x_buf,
    slope_even,
    slope_odd,
    keep_even,
    keep_odd,
    w_high,
    w_low,
    pooled,
    pooled_x,
    w_sem,
    x_sem,
    slope_sem,
):
    core = place_ref[0]
    w_copies = [
        pltpu.make_async_copy(ref.at[:, core], buf, w_sem.at[i])
        for i, (ref, buf) in enumerate(((w_in_ref, w_in_buf), (w_out_ref, w_out_buf)))
    ]
    x_copies = [pltpu.make_async_copy(ref, x_buf.at[i], x_sem.at[i]) for i, ref in enumerate((own_ref, other_ref))]
    w_copies[0].start()
    x_copies[0].start()
    w_copies[0].wait()
    x_copies[1].start()
    w_copies[1].start()
    for z in range(N_Z):
        rows = slice(z * BLOCK, (z + 1) * BLOCK)
        w_high[rows], w_low[rows] = split(w_in_buf[z] * gain_ref[...])
    position = iota((LMAX, 1), 0)

    keeps, slope_bufs = (keep_even, keep_odd), (slope_even, slope_odd)

    def store_from(buf, parity, step):
        rows = slice(step * TOKENS, (step + 1) * TOKENS)
        return pltpu.make_async_copy(buf, slope_ref.at[rows], slope_sem.at[parity])

    def tokens_of(step):
        start = step % (STEPS // 2) * TOKENS
        return x_buf[step // (STEPS // 2), start : start + TOKENS]

    def product(step, keep):
        x = tokens_of(step)
        for j in range(HALF // 256):
            cols = slice(j * 256, (j + 1) * 256)
            keep[:, cols] = dot(x, w_high[cols], NT) + dot(x, w_low[cols], NT)

    def turn(step, now, later, slope_out, copy):
        if step >= 2:
            copy(step - 2).wait()
        if step + 1 < STEPS:
            product(step + 1, later)
        xf = tokens_of(step).astype(f32)
        inverse = lax.rsqrt(jnp.sum(xf * xf, axis=1, keepdims=True) * (1.0 / D) + 1e-05)
        weights = []
        for i in range(TEXTS_STEP):
            length = lengths_ref[step * TEXTS_STEP + i]
            scale = 1.0 / jnp.full((1, 1), length, jnp.int32).astype(f32)
            weights.append(jnp.where(position < length, scale, 0.0))
            rows = slice(i * LMAX, (i + 1) * LMAX)
            pooled_x[step, i : i + 1] = jnp.sum(xf[rows] * weights[i], axis=0, keepdims=True)
        weight = jnp.concatenate(weights, axis=0)
        scaled = weight * inverse
        for j in range(HALF // 256):
            cols = slice(j * 256, (j + 1) * 256)
            p = now[:, cols] * inverse
            p2 = p * p
            half = 0.5 + 0.5 * jnp.tanh(p * (C0 + C1 * p2))
            act = p * half
            slope = half + (act - act * half) * (2.0 * C0 + 6.0 * C1 * p2)
            slope_out[:, cols] = slope * scaled
            act = act * weight
            for i in range(TEXTS_STEP):
                rows = slice(i * LMAX, (i + 1) * LMAX)
                pooled[step, i : i + 1, cols] = jnp.sum(act[rows], axis=0, keepdims=True)
        copy(step).start()

    x_copies[0].wait()
    product(0, keeps[0])
    for step in range(STEPS):
        if step == STEPS // 2 - 1:
            x_copies[1].wait()
        parity = step % 2
        store = functools.partial(store_from, slope_bufs[parity], parity)
        turn(step, keeps[parity], keeps[1 - parity], slope_bufs[parity], store)
    w_copies[1].wait()
    acts = jnp.concatenate([pooled[i] for i in range(STEPS)], axis=0)
    total = 0.5 * jnp.concatenate([pooled_x[i] for i in range(STEPS)], axis=0)
    for z in range(N_Z):
        high, low = split(w_out_buf[z])
        out_high_ref[z] = high
        out_low_ref[z] = low
        a = acts[:, z * BLOCK : (z + 1) * BLOCK]
        pooled_ref[z] = jnp.concatenate([a, jnp.zeros((2 * TXT, 256 - BLOCK), f32)], axis=1)
        a_high, a_low = split(a)
        total = total + (dot(a_high, high, NN) + (dot(a_high, low, NN) + dot(a_low, high, NN)))
    sums_ref[...] = total
    for parity in range(2):
        store_from(slope_bufs[parity], parity, STEPS - 2 + parity).wait()


def forward(place, lengths, gain, own, other, w_in, w_out):
    tokens = 2 * TXT * LMAX
    shape = jax.ShapeDtypeStruct
    return pl.pallas_call(
        forward_kernel,
        out_shape=(
            pltpu.HBM((tokens, HALF), f32),
            shape((N_Z, 2 * TXT, 256), f32),
            shape((2 * TXT, D), f32),
            shape((N_Z, BLOCK, D), bf16),
            shape((N_Z, BLOCK, D), bf16),
        ),
        in_specs=smem(2) + vmem(1) + [HBM] * 4,
        out_specs=(HBM, *vmem(4)),
        scratch_shapes=[
            pltpu.VMEM((N_Z, BLOCK, D), f32),
            pltpu.VMEM((N_Z, BLOCK, D), f32),
            pltpu.VMEM((2, TXT * LMAX, D), bf16),
            pltpu.VMEM((TOKENS, HALF), f32),
            pltpu.VMEM((TOKENS, HALF), f32),
            pltpu.VMEM((TOKENS, HALF), f32),
            pltpu.VMEM((TOKENS, HALF), f32),
            pltpu.VMEM((HALF, D), bf16),
            pltpu.VMEM((HALF, D), bf16),
            pltpu.VMEM((STEPS, TEXTS_STEP, HALF), f32),
            pltpu.VMEM((STEPS, TEXTS_STEP, D), f32),
            pltpu.SemaphoreType.DMA((2,)),
            pltpu.SemaphoreType.DMA((2,)),
            pltpu.SemaphoreType.DMA((2,)),
        ],
        compiler_params=params(24),
        cost_estimate=cost(10 * tokens * HALF * D, 8 * 10**6),
        name="encoder_forward",
    )(place, lengths, gain, in_hbm(own), in_hbm(other), in_hbm(w_in), in_hbm(w_out))


def unit_rows(sums):
    return lax.rsqrt(jnp.sum(sums * sums, axis=-1, keepdims=True) + 1e-06)


def each_label(owners_ref, counts, put):
    for o in range(N_LABEL):
        counts[o] = 0
    for i in range(TXT):
        owner = owners_ref[i]
        rank = counts[owner]
        counts[owner] = rank + 1
        put(i, owner, jnp.minimum(rank, CAP - 1))


def label_kernel(owners_ref, part_ref, came_ref, free_ref, sums_ref, out_ref, counts):
    own = part_ref[:TXT] + came_ref[TXT:]
    sums_ref[:TXT] = own
    sums_ref[TXT:] = part_ref[TXT:] + came_ref[:TXT]
    scaled = (own * unit_rows(own) + free_ref[...]) * LABEL_SCALE
    out_ref[...] = jnp.zeros_like(out_ref)

    def put(i, owner, rank):
        first = owner // 8 * (8 * SLOT_ROWS) + rank * (8 * PIECES) + lax.rem(owner, 8)
        for j in range(PIECES):
            out_ref[pl.ds(first + 8 * j, 1)] = scaled[i : i + 1, j * 128 : (j + 1) * 128]

    each_label(owners_ref, counts, put)


def labels(owners, part, came, free_vectors):
    return pl.pallas_call(
        label_kernel,
        out_shape=(
            jax.ShapeDtypeStruct((2 * TXT, D), f32),
            jax.ShapeDtypeStruct((N_LABEL * SLOT_ROWS, 128), f32),
        ),
        in_specs=smem(1) + vmem(3),
        out_specs=tuple(vmem(2)),
        scratch_shapes=[pltpu.SMEM((N_LABEL,), jnp.int32)],
        compiler_params=params(8),
        cost_estimate=cost(10**6, 8 * 10**5),
        name="label_vectors",
    )(owners, part, came, free_vectors)


def scores_kernel(place_ref, shortlist_ref, queries_ref, own_ref, other_ref, out_ref):
    size = 2 * CHIP_SLOTS
    column = iota((size, size), 0)
    rank = column % CAP
    lab = column // CAP % N_LABEL
    core = column // (CAP * N_LABEL) % N_CORE
    z = column // (CAP * N_LABEL * N_CORE)
    half = jnp.where(core == place_ref[0], 0, 1)
    source = half * CHIP_SLOTS + rank * N_CHIPS + z * N_LABEL + lab
    order = (iota((size, size), 1) == source).astype(bf16)
    table = jnp.concatenate(
        [
            jnp.concatenate(
                [ref[pl.ds(PIECES * r + j, N_CHIPS, stride=SLOT_ROWS)] for j in range(PIECES)],
                axis=1,
            )
            for ref in (own_ref, other_ref)
            for r in range(CAP)
        ],
        axis=0,
    )
    t_high, t_low = (dot(order, part, NN).astype(bf16) for part in split(table))
    q_high, q_low = split(queries_ref[...])
    scores = dot(q_high, t_high, NT) + (dot(q_high, t_low, NT) + dot(q_low, t_high, NT))
    out_ref[...] = scores * is_kept(shortlist_ref, place_ref[1])


def slot_scores(place, shortlist, queries, own, other):
    return pl.pallas_call(
        scores_kernel,
        out_shape=jax.ShapeDtypeStruct((QROWS, 2 * CHIP_SLOTS), f32),
        in_specs=smem(1) + vmem(4),
        out_specs=pl.BlockSpec(memory_space=pltpu.VMEM),
        compiler_params=params(24),
        cost_estimate=cost(6 * QROWS * 256 * D, 4 * 10**6),
        name="slot_scores",
    )(place, shortlist, queries, own, other)


def return_kernel(owners_ref, came_ref, out_ref, again_ref, counts):
    def put(i, owner, rank):
        value = came_ref[owner]
        for z in range(1, N_Z):
            value = value + came_ref[z * N_LABEL + owner]
        value = jnp.where(rank == 0, value[:PIECES], value[PIECES : 2 * PIECES])
        for j in range(PIECES):
            out_ref[i : i + 1, j * 128 : (j + 1) * 128] = value[j : j + 1]
            again_ref[i : i + 1, j * 128 : (j + 1) * 128] = value[j : j + 1]

    each_label(owners_ref, counts, put)


def returned(owners, came):
    return pl.pallas_call(
        return_kernel,
        out_shape=(jax.ShapeDtypeStruct((TXT, D), f32),) * 2,
        in_specs=smem(1) + vmem(1),
        out_specs=tuple(vmem(2)),
        scratch_shapes=[pltpu.SMEM((N_LABEL,), jnp.int32)],
        compiler_params=params(8),
        cost_estimate=cost(10**5, 5 * 10**5),
        name="returned_gradients",
    )(owners, came)


def pull_kernel(place_ref, free_own_ref, free_other_ref, sums_ref, high_ref, low_ref, pooled_ref, labels_ref, back_ref, *outs):
    free = jnp.concatenate([free_own_ref[...], free_other_ref[...]], axis=0)
    sums = sums_ref[...]
    unit = unit_rows(sums)
    along = jnp.sum(sums * free, axis=-1, keepdims=True)
    pulled = unit * free - (unit * unit * unit * along) * sums
    p_high, p_low = split(pulled)
    back_ref[...] = jnp.concatenate(
        [
            dot(p_high, high_ref[z], NT) + (dot(p_high, low_ref[z], NT) + dot(p_low, high_ref[z], NT))
            for z in range(N_Z)
        ],
        axis=1,
    )
    for f in range(N_Z):
        acts = pooled_ref[lax.rem(place_ref[4] + f, N_Z)]
        for k in range(FACTOR_ROWS // (2 * TXT)):
            piece = acts[:, k * 128 : (k + 1) * 128] if k < 2 else pulled[:, (k - 2) * 128 : (k - 1) * 128]
            outs[f][k * 2 * TXT : (k + 1) * 2 * TXT] = piece
        outs[f][FACTOR_ROWS:] = labels_ref[...]


def pull(place, free_own, free_other, sums, high, low, pooled, label_rows):
    return pl.pallas_call(
        pull_kernel,
        out_shape=(jax.ShapeDtypeStruct((2 * TXT, HALF), f32),)
        + (jax.ShapeDtypeStruct((MOVED_ROWS, 128), f32),) * N_Z,
        in_specs=smem(1) + vmem(7),
        out_specs=tuple(vmem(1 + N_Z)),
        compiler_params=params(12),
        cost_estimate=cost(6 * 32 * HALF * D, 3 * 10**6),
        name="pull_back",
    )(place, free_own, free_other, sums, high, low, pooled, label_rows)


def backward_kernel(back_ref, gain_ref, own_ref, other_ref, slope_ref, grad, largest, x_buf, slope_buf, sem):
    copies = []
    for q in range(PARTS):
        x_rows = slice(q % (PARTS // 2) * PART, (q % (PARTS // 2) + 1) * PART)
        x_ref = (own_ref, other_ref)[q // (PARTS // 2)]
        rows = slice(q * PART, (q + 1) * PART)
        copies.append(
            (
                pltpu.make_async_copy(x_ref.at[x_rows], x_buf.at[q], sem.at[0, q]),
                pltpu.make_async_copy(slope_ref.at[rows], slope_buf.at[q], sem.at[1, q]),
            )
        )
    for copy in copies[0]:
        copy.start()
    for q in range(PARTS):
        for copy in copies[q]:
            copy.wait()
        if q + 1 < PARTS:
            for copy in copies[q + 1]:
                copy.start()

        def product(j):
            cols = slice(j * 256, (j + 1) * 256)
            total = jnp.zeros((256, D), f32)
            for i in range(PART // TOKENS):
                pieces = []
                for t in range(i * TEXTS_STEP, (i + 1) * TEXTS_STEP):
                    text = q * (PART // LMAX) + t
                    pieces.append(slope_buf[q, t * LMAX : (t + 1) * LMAX, cols] * back_ref[text : text + 1, cols])
                high, low = split(jnp.concatenate(pieces, axis=0))
                x = x_buf[q, i * TOKENS : (i + 1) * TOKENS]
                total = total + (dot(high, x, TN) + dot(low, x, TN))
            if q > 0:
                total = total + grad[cols]
            if q == PARTS - 1:
                total = total * gain_ref[...]
                largest[j : j + 1] = jnp.max(jnp.abs(total), axis=0, keepdims=True)
            grad[cols] = total

        for j in range(HALF // 256):
            product(j)


def backward(back, gain, own, other, slope):
    tokens = 2 * TXT * LMAX
    shape = jax.ShapeDtypeStruct
    return pl.pallas_call(
        backward_kernel,
        out_shape=(shape((HALF, D), f32), shape((HALF // 256, D), f32)),
        in_specs=vmem(2) + [HBM] * 3,
        out_specs=tuple(vmem(2)),
        scratch_shapes=[
            pltpu.VMEM((PARTS, PART, D), bf16),
            pltpu.VMEM((PARTS, PART, HALF), f32),
            pltpu.SemaphoreType.DMA((2, PARTS)),
        ],
        compiler_params=params(24),
        cost_estimate=cost(5 * tokens * HALF * D, 4 * 10**6),
        name="encoder_backward",
    )(back, gain, in_hbm(own), in_hbm(other), in_hbm(slope))


def power_of(top):
    return jnp.clip(jnp.floor(14.0 - jnp.log2(jnp.maximum(top, 1e-30))), -100.0, 100.0)


def finish_kernel(grad_ref, largest_ref, *rest):
    factors, out_ref = rest[:N_Z], rest[N_Z]
    wide = jnp.concatenate(
        [
            jnp.concatenate([ref[k * 2 * TXT : (k + 1) * 2 * TXT] for ref in factors], axis=0)
            for k in range(FACTOR_ROWS // (2 * TXT))
        ],
        axis=1,
    )
    block = dot3(wide[:, :BLOCK], wide[:, 256:], TN)
    top = jnp.max(jnp.max(largest_ref[...], axis=0, keepdims=True), axis=1, keepdims=True)
    block_top = jnp.max(jnp.max(jnp.abs(block), axis=0, keepdims=True), axis=1, keepdims=True)
    power, block_power = power_of(top), power_of(block_top)
    scale = jnp.exp2(power)
    block = block * jnp.exp2(block_power)
    powers = jnp.where(iota((8, 128), 0) < 4, power, block_power)
    for lab in range(N_LABEL):
        first = lab * SENT_ROWS
        for j in range(PIECES):
            start = first + AT_W_OUT + j * ROWS
            out_ref[start : start + ROWS] = block[lab * ROWS : (lab + 1) * ROWS, j * 128 : (j + 1) * 128]
        out_ref[first + AT_POWERS : first + AT_LABELS] = powers
    for f in range(N_Z):
        for g in range(N_LABEL // 8):
            for k in range(SLOT_ROWS):
                start = g * 8 * SENT_ROWS + AT_LABELS + f * SLOT_ROWS + k
                row = FACTOR_ROWS + (g * SLOT_ROWS + k) * 8
                out_ref[pl.ds(start, 8, stride=SENT_ROWS)] = factors[f][row : row + 8]
    for z in range(N_Z):
        for k in range(N_LABEL // 2):
            start = z * BLOCK + k * 2 * ROWS
            rows = grad_ref[start : start + 2 * ROWS] * scale
            for g in range(2):
                for j in range(PIECES):
                    piece = rows[g * ROWS : (g + 1) * ROWS, j * 128 : (j + 1) * 128]
                    first = (2 * k + g) * SENT_ROWS + z * CHUNK + j * ROWS
                    out_ref[first : first + ROWS] = piece


def finish(grad, largest, factors):
    return pl.pallas_call(
        finish_kernel,
        out_shape=jax.ShapeDtypeStruct((N_LABEL * SENT_ROWS, 128), f32),
        in_specs=vmem(2 + N_Z),
        out_specs=pl.BlockSpec(memory_space=pltpu.VMEM),
        compiler_params=params(16),
        cost_estimate=cost(10**9, 5 * 10**6),
        name="finish_gradients",
    )(grad, largest, *factors)


def unpieced(rows):
    return jnp.concatenate([rows[j * ROWS : (j + 1) * ROWS] for j in range(PIECES)], axis=1)


def middle_kernel(place_ref, came_ref, w_out_ref, table_ref, *outs):
    total = jnp.zeros((AT_W_OUT, 128), f32)
    block = jnp.zeros((CHUNK, 128), f32)
    for lab in range(N_LABEL):
        total = total + came_ref[lab, :AT_W_OUT] * jnp.exp2(-came_ref[lab, AT_POWERS : AT_POWERS + 1])
        block = block + came_ref[lab, AT_W_OUT:AT_POWERS] * jnp.exp2(-came_ref[lab, AT_POWERS + 4 : AT_POWERS + 5])
    w_out_ref[...] = unpieced(block)
    for f in range(N_Z):
        z = lax.rem(place_ref[4] - f + N_Z, N_Z)
        for lab in range(N_LABEL):
            first = AT_LABELS + f * SLOT_ROWS
            table_ref[z, lab * SLOT_ROWS : (lab + 1) * SLOT_ROWS] = came_ref[lab, first : first + SLOT_ROWS] * (
                1.0 / LABEL_SCALE
            )
    for z in range(N_Z):
        for f in range(N_Z):

            @pl.when(lax.rem(place_ref[4] + f, N_Z) == z)
            def _(z=z, f=f):
                outs[f][...] = total[z * CHUNK : (z + 1) * CHUNK]


def middle(place, came):
    return pl.pallas_call(
        middle_kernel,
        out_shape=(
            jax.ShapeDtypeStruct((ROWS, D), f32),
            jax.ShapeDtypeStruct((N_Z, N_LABEL * SLOT_ROWS, 128), f32),
        )
        + (jax.ShapeDtypeStruct((CHUNK, 128), f32),) * N_Z,
        in_specs=smem(1) + vmem(1),
        out_specs=tuple(vmem(2 + N_Z)),
        compiler_params=params(16),
        cost_estimate=cost(10**7, 4 * 10**6),
        name="plane_sums",
    )(place, came)


def last_kernel(*rest):
    blocks, w_in_ref = rest[:N_Z], rest[-1]
    w_in_ref[...] = unpieced((blocks[0][...] + blocks[1][...]) + (blocks[2][...] + blocks[3][...]))


def last(blocks, after):
    return pl.pallas_call(
        last_kernel,
        out_shape=jax.ShapeDtypeStruct((ROWS, D), f32),
        in_specs=vmem(N_Z) + [HBM],
        out_specs=pl.BlockSpec(memory_space=pltpu.VMEM),
        compiler_params=params(8),
        cost_estimate=cost(10**6, 10**6),
        name="z_sums",
    )(*blocks, in_hbm(after))


def swap(value):
    return lax.ppermute(value, "core", ((0, 1), (1, 0)))


def shift(blocks, axis):
    moved = [lax.ppermute(blocks[k], axis, [(i, (i + k) % 4) for i in range(4)]) for k in range(1, 4)]
    return [blocks[0]] + moved


def exchange(value, axes):
    return lax.all_to_all(value, axes, split_axis=0, concat_axis=0, tiled=True)


def local(texts, lengths, owners, gain, w_in, w_out, free_vectors, queries, shortlist, grad_scores):
    core, x, y, z = (lax.axis_index(name) for name in ("core", "x", "y", "z"))
    place = jnp.stack([core, x * N_Y + y, x, y, z]).astype(jnp.int32)
    own = texts.reshape(TXT * LMAX, D)
    other = swap(own)
    both_lengths = jnp.concatenate([lengths, swap(lengths)])
    owner_ids = owners[:, 0]
    names = shortlist.T
    gain_row = gain.reshape(1, D)
    w_in_blocks = w_in.reshape(N_Z, N_CORE, BLOCK, D)
    w_out_blocks = w_out.reshape(N_Z, N_CORE, BLOCK, D)

    kept, sent = slot_partials(place, names, grad_scores, queries)
    slots = exchange((kept + swap(sent)).reshape(N_CHIPS, 16, 128), ("z", "x", "y"))

    slope, pooled, part, high, low = forward(place, both_lengths, gain_row, own, other, w_in_blocks, w_out_blocks)
    sums, label_rows = labels(owner_ids, part, swap(part), free_vectors)

    free_grad, free_own = returned(owner_ids, slots)
    back, *factors = pull(place, free_own, swap(free_own), sums, high, low, pooled, label_rows)
    factors = shift(factors, "z")
    grad, largest = backward(back, gain_row, own, other, slope)
    sent_rows = finish(grad, largest, factors).reshape(N_LABEL, SENT_ROWS, 128)
    came = exchange(sent_rows.astype(jnp.float16), LABEL).astype(f32)
    w_out_grad, table, *moved = middle(place, came)
    table = table.reshape(N_CHIPS * SLOT_ROWS, 128)
    moved = shift(moved, "z")
    scores = slot_scores(place, names, queries, table, swap(table))
    w_in_grad = last(moved, scores)
    return scores, free_grad, w_in_grad, w_out_grad


def solution(mesh):
    fine = Mesh(mesh.devices.reshape(N_Z, N_CORE, N_X, N_Y), ("z", "core", "x", "y"))
    dp, every = ("z", "core"), ("z", "core", "x", "y")
    placed = (
        P(every, None, None),
        P(every),
        P(every, None),
        P(),
        P(),
        P(),
        P(every, None),
        P(dp, None),
        P(dp, None),
        P(dp, LABEL),
    )
    return jax.shard_map(
        local,
        mesh=fine,
        in_specs=placed,
        out_specs=(
            P(dp, LABEL),
            P(every, None),
            P(every, None),
            P(every, None),
        ),
        check_vma=False,
    )
```

```python
import functools
import math

import jax
import jax.numpy as jnp
from jax import lax
from jax.experimental import pallas as pl
from jax.experimental.pallas import tpu as pltpu
from jax.sharding import Mesh, PartitionSpec as P

N_Z, N_CORE, N_X, N_Y = 4, 2, 4, 4
N_LABEL = N_X * N_Y
TXT = 16
LMAX = 64
D = 768
FF = 1536
HALF = FF // 2
BLOCK = FF // (N_Z * N_CORE)
ROWS = BLOCK // N_LABEL
CAP = 2
SLOTS = N_LABEL * CAP
QROWS = 512
TOKENS = 256
TEXTS_STEP = TOKENS // LMAX
STEPS = 2 * TXT // TEXTS_STEP
C0 = math.sqrt(2.0 / math.pi)
C1 = C0 * 0.044715
MIB = 1024 * 1024

f32 = jnp.float32
bf16 = jnp.bfloat16
N_CHIPS = N_Z * N_LABEL
CHIP_SLOTS = N_CHIPS * CAP
PIECES = D // 128
CHUNK = PIECES * ROWS
SLOT_ROWS = CAP * PIECES
AT_W_OUT = N_Z * CHUNK
AT_POWERS = AT_W_OUT + CHUNK
AT_LABELS = AT_POWERS + 8
SENT_ROWS = AT_LABELS + N_Z * SLOT_ROWS
FACTOR_ROWS = 2 * TXT * (256 + D) // 128
MOVED_ROWS = FACTOR_ROWS + N_LABEL * SLOT_ROWS
LABEL_SCALE = 256.0
PARTS = 2
PART = 2 * TXT * LMAX // PARTS
LABEL = ("x", "y")


def split(value):
    high = value.astype(bf16)
    return high, (value - high.astype(f32)).astype(bf16)


def dot(a, b, dims):
    return lax.dot_general(a, b, (dims, ((), ())), preferred_element_type=f32)


def dot3(a, b, dims):
    a_high, a_low = split(a)
    b_high, b_low = split(b)
    return dot(a_high, b_high, dims) + (dot(a_high, b_low, dims) + dot(a_low, b_high, dims))


def params(mib):
    return pltpu.CompilerParams(vmem_limit_bytes=mib * MIB)


def vmem(count):
    return [pl.BlockSpec(memory_space=pltpu.VMEM)] * count


def smem(count):
    return [pl.BlockSpec(memory_space=pltpu.SMEM)] * count


def is_kept(shortlist_ref, label):
    row = jnp.max((shortlist_ref[...] == label).astype(f32), axis=0, keepdims=True)
    return jnp.broadcast_to(row, (8, QROWS)).T[:, :1]


def iota(shape, axis):
    return lax.broadcasted_iota(jnp.int32, shape, axis)


def in_hbm(value):
    return pltpu.with_memory_space_constraint(value, pltpu.HBM)


def cost(flops, nbytes):
    return pl.CostEstimate(flops=flops, bytes_accessed=nbytes, transcendentals=0)


ANY = pl.BlockSpec(memory_space=pl.ANY)
HBM = pl.BlockSpec(memory_space=pltpu.HBM)
NN, NT, TN = ((1,), (0,)), ((1,), (1,)), ((0,), (0,))


def partial_kernel(place_ref, shortlist_ref, grad_ref, queries_ref, own_ref, other_ref):
    weighted = grad_ref[...] * is_kept(shortlist_ref, place_ref[1])
    size = 2 * CHIP_SLOTS
    target = iota((size, size), 1)
    half = target // CHIP_SLOTS
    rank = target // N_CHIPS % CAP
    z = target // N_LABEL % N_Z
    lab = target % N_LABEL
    flip = jnp.where(half == 0, place_ref[0], 1 - place_ref[0])
    source = ((z * N_CORE + flip) * N_LABEL + lab) * CAP + rank
    order = (iota((size, size), 0) == source).astype(bf16)
    w_high, w_low = (dot(part, order, NN).astype(bf16) for part in split(weighted))
    q_high, q_low = split(queries_ref[...])
    total = dot(w_high, q_high, TN) + (dot(w_high, q_low, TN) + dot(w_low, q_high, TN))
    for h, ref in enumerate((own_ref, other_ref)):
        for r in range(CAP):
            start = h * CHIP_SLOTS + r * N_CHIPS
            for j in range(PIECES):
                ref[pl.ds(PIECES * r + j, N_CHIPS, stride=16)] = total[start : start + N_CHIPS, j * 128 : (j + 1) * 128]


def slot_partials(place, shortlist, grad_scores, queries):
    shape = jax.ShapeDtypeStruct((N_CHIPS * 16, 128), f32)
    return pl.pallas_call(
        partial_kernel,
        out_shape=(shape, shape),
        in_specs=smem(1) + vmem(3),
        out_specs=tuple(vmem(2)),
        compiler_params=params(24),
        cost_estimate=cost(6 * QROWS * 256 * D, 4 * 10**6),
        name="slot_partials",
    )(place, in_hbm(shortlist), in_hbm(grad_scores), in_hbm(queries))


def forward_kernel(
    place_ref,
    lengths_ref,
    gain_ref,
    own_ref,
    other_ref,
    w_in_ref,
    w_out_ref,
    slope_ref,
    pooled_ref,
    sums_ref,
    out_high_ref,
    out_low_ref,
    w_in_buf,
    w_out_buf,
    x_buf,
    slope_even,
    slope_odd,
    keep_even,
    keep_odd,
    w_high,
    w_low,
    pooled,
    pooled_x,
    w_sem,
    x_sem,
    slope_sem,
):
    core = place_ref[0]
    w_copies = [
        pltpu.make_async_copy(ref.at[:, core], buf, w_sem.at[i])
        for i, (ref, buf) in enumerate(((w_in_ref, w_in_buf), (w_out_ref, w_out_buf)))
    ]
    x_copies = [pltpu.make_async_copy(ref, x_buf.at[i], x_sem.at[i]) for i, ref in enumerate((own_ref, other_ref))]
    w_copies[0].start()
    x_copies[0].start()
    w_copies[0].wait()
    x_copies[1].start()
    w_copies[1].start()
    for z in range(N_Z):
        rows = slice(z * BLOCK, (z + 1) * BLOCK)
        w_high[rows], w_low[rows] = split(w_in_buf[z] * gain_ref[...])
    position = iota((LMAX, 1), 0)

    keeps, slope_bufs = (keep_even, keep_odd), (slope_even, slope_odd)

    def store_from(buf, parity, step):
        rows = slice(step * TOKENS, (step + 1) * TOKENS)
        return pltpu.make_async_copy(buf, slope_ref.at[rows], slope_sem.at[parity])

    def tokens_of(step):
        start = step % (STEPS // 2) * TOKENS
        return x_buf[step // (STEPS // 2), start : start + TOKENS]

    def product(step, keep):
        x = tokens_of(step)
        for j in range(HALF // 256):
            cols = slice(j * 256, (j + 1) * 256)
            keep[:, cols] = dot(x, w_high[cols], NT) + dot(x, w_low[cols], NT)

    def turn(step, now, later, slope_out, copy):
        if step >= 2:
            copy(step - 2).wait()
        if step + 1 < STEPS:
            product(step + 1, later)
        xf = tokens_of(step).astype(f32)
        inverse = lax.rsqrt(jnp.sum(xf * xf, axis=1, keepdims=True) * (1.0 / D) + 1e-05)
        weights = []
        for i in range(TEXTS_STEP):
            length = lengths_ref[step * TEXTS_STEP + i]
            scale = 1.0 / jnp.full((1, 1), length, jnp.int32).astype(f32)
            weights.append(jnp.where(position < length, scale, 0.0))
            rows = slice(i * LMAX, (i + 1) * LMAX)
            pooled_x[step, i : i + 1] = jnp.sum(xf[rows] * weights[i], axis=0, keepdims=True)
        weight = jnp.concatenate(weights, axis=0)
        scaled = weight * inverse
        for j in range(HALF // 256):
            cols = slice(j * 256, (j + 1) * 256)
            p = now[:, cols] * inverse
            p2 = p * p
            half = 0.5 + 0.5 * jnp.tanh(p * (C0 + C1 * p2))
            act = p * half
            slope = half + (act - act * half) * (2.0 * C0 + 6.0 * C1 * p2)
            slope_out[:, cols] = slope * scaled
            act = act * weight
            for i in range(TEXTS_STEP):
                rows = slice(i * LMAX, (i + 1) * LMAX)
                pooled[step, i : i + 1, cols] = jnp.sum(act[rows], axis=0, keepdims=True)
        copy(step).start()

    x_copies[0].wait()
    product(0, keeps[0])
    for step in range(STEPS):
        if step == STEPS // 2 - 1:
            x_copies[1].wait()
        parity = step % 2
        store = functools.partial(store_from, slope_bufs[parity], parity)
        turn(step, keeps[parity], keeps[1 - parity], slope_bufs[parity], store)
    w_copies[1].wait()
    acts = jnp.concatenate([pooled[i] for i in range(STEPS)], axis=0)
    total = 0.5 * jnp.concatenate([pooled_x[i] for i in range(STEPS)], axis=0)
    for z in range(N_Z):
        high, low = split(w_out_buf[z])
        out_high_ref[z] = high
        out_low_ref[z] = low
        a = acts[:, z * BLOCK : (z + 1) * BLOCK]
        pooled_ref[z] = jnp.concatenate([a, jnp.zeros((2 * TXT, 256 - BLOCK), f32)], axis=1)
        a_high, a_low = split(a)
        total = total + (dot(a_high, high, NN) + (dot(a_high, low, NN) + dot(a_low, high, NN)))
    sums_ref[...] = total
    for parity in range(2):
        store_from(slope_bufs[parity], parity, STEPS - 2 + parity).wait()


def forward(place, lengths, gain, own, other, w_in, w_out):
    tokens = 2 * TXT * LMAX
    shape = jax.ShapeDtypeStruct
    return pl.pallas_call(
        forward_kernel,
        out_shape=(
            pltpu.HBM((tokens, HALF), f32),
            shape((N_Z, 2 * TXT, 256), f32),
            shape((2 * TXT, D), f32),
            shape((N_Z, BLOCK, D), bf16),
            shape((N_Z, BLOCK, D), bf16),
        ),
        in_specs=smem(2) + vmem(1) + [HBM] * 4,
        out_specs=(HBM, *vmem(4)),
        scratch_shapes=[
            pltpu.VMEM((N_Z, BLOCK, D), f32),
            pltpu.VMEM((N_Z, BLOCK, D), f32),
            pltpu.VMEM((2, TXT * LMAX, D), bf16),
            pltpu.VMEM((TOKENS, HALF), f32),
            pltpu.VMEM((TOKENS, HALF), f32),
            pltpu.VMEM((TOKENS, HALF), f32),
            pltpu.VMEM((TOKENS, HALF), f32),
            pltpu.VMEM((HALF, D), bf16),
            pltpu.VMEM((HALF, D), bf16),
            pltpu.VMEM((STEPS, TEXTS_STEP, HALF), f32),
            pltpu.VMEM((STEPS, TEXTS_STEP, D), f32),
            pltpu.SemaphoreType.DMA((2,)),
            pltpu.SemaphoreType.DMA((2,)),
            pltpu.SemaphoreType.DMA((2,)),
        ],
        compiler_params=params(24),
        cost_estimate=cost(10 * tokens * HALF * D, 8 * 10**6),
        name="encoder_forward",
    )(place, lengths, gain, in_hbm(own), in_hbm(other), in_hbm(w_in), in_hbm(w_out))


def unit_rows(sums):
    return lax.rsqrt(jnp.sum(sums * sums, axis=-1, keepdims=True) + 1e-06)


def each_label(owners_ref, counts, put):
    for o in range(N_LABEL):
        counts[o] = 0
    for i in range(TXT):
        owner = owners_ref[i]
        rank = counts[owner]
        counts[owner] = rank + 1
        put(i, owner, jnp.minimum(rank, CAP - 1))


def label_kernel(owners_ref, part_ref, came_ref, free_ref, sums_ref, out_ref, counts):
    own = part_ref[:TXT] + came_ref[TXT:]
    sums_ref[:TXT] = own
    sums_ref[TXT:] = part_ref[TXT:] + came_ref[:TXT]
    scaled = (own * unit_rows(own) + free_ref[...]) * LABEL_SCALE
    out_ref[...] = jnp.zeros_like(out_ref)

    def put(i, owner, rank):
        first = owner // 8 * (8 * SLOT_ROWS) + rank * (8 * PIECES) + lax.rem(owner, 8)
        for j in range(PIECES):
            out_ref[pl.ds(first + 8 * j, 1)] = scaled[i : i + 1, j * 128 : (j + 1) * 128]

    each_label(owners_ref, counts, put)


def labels(owners, part, came, free_vectors):
    return pl.pallas_call(
        label_kernel,
        out_shape=(
            jax.ShapeDtypeStruct((2 * TXT, D), f32),
            jax.ShapeDtypeStruct((N_LABEL * SLOT_ROWS, 128), f32),
        ),
        in_specs=smem(1) + vmem(3),
        out_specs=tuple(vmem(2)),
        scratch_shapes=[pltpu.SMEM((N_LABEL,), jnp.int32)],
        compiler_params=params(8),
        cost_estimate=cost(10**6, 8 * 10**5),
        name="label_vectors",
    )(owners, part, came, free_vectors)


def scores_kernel(place_ref, shortlist_ref, queries_ref, own_ref, other_ref, out_ref):
    size = 2 * CHIP_SLOTS
    column = iota((size, size), 0)
    rank = column % CAP
    lab = column // CAP % N_LABEL
    core = column // (CAP * N_LABEL) % N_CORE
    z = column // (CAP * N_LABEL * N_CORE)
    half = jnp.where(core == place_ref[0], 0, 1)
    source = half * CHIP_SLOTS + rank * N_CHIPS + z * N_LABEL + lab
    order = (iota((size, size), 1) == source).astype(bf16)
    table = jnp.concatenate(
        [
            jnp.concatenate(
                [ref[pl.ds(PIECES * r + j, N_CHIPS, stride=SLOT_ROWS)] for j in range(PIECES)],
                axis=1,
            )
            for ref in (own_ref, other_ref)
            for r in range(CAP)
        ],
        axis=0,
    )
    t_high, t_low = (dot(order, part, NN).astype(bf16) for part in split(table))
    q_high, q_low = split(queries_ref[...])
    scores = dot(q_high, t_high, NT) + (dot(q_high, t_low, NT) + dot(q_low, t_high, NT))
    out_ref[...] = scores * is_kept(shortlist_ref, place_ref[1])


def slot_scores(place, shortlist, queries, own, other):
    return pl.pallas_call(
        scores_kernel,
        out_shape=jax.ShapeDtypeStruct((QROWS, 2 * CHIP_SLOTS), f32),
        in_specs=smem(1) + vmem(4),
        out_specs=pl.BlockSpec(memory_space=pltpu.VMEM),
        compiler_params=params(24),
        cost_estimate=cost(6 * QROWS * 256 * D, 4 * 10**6),
        name="slot_scores",
    )(place, shortlist, queries, own, other)


def return_kernel(owners_ref, came_ref, out_ref, again_ref, counts):
    def put(i, owner, rank):
        value = came_ref[owner]
        for z in range(1, N_Z):
            value = value + came_ref[z * N_LABEL + owner]
        value = jnp.where(rank == 0, value[:PIECES], value[PIECES : 2 * PIECES])
        for j in range(PIECES):
            out_ref[i : i + 1, j * 128 : (j + 1) * 128] = value[j : j + 1]
            again_ref[i : i + 1, j * 128 : (j + 1) * 128] = value[j : j + 1]

    each_label(owners_ref, counts, put)


def returned(owners, came):
    return pl.pallas_call(
        return_kernel,
        out_shape=(jax.ShapeDtypeStruct((TXT, D), f32),) * 2,
        in_specs=smem(1) + vmem(1),
        out_specs=tuple(vmem(2)),
        scratch_shapes=[pltpu.SMEM((N_LABEL,), jnp.int32)],
        compiler_params=params(8),
        cost_estimate=cost(10**5, 5 * 10**5),
        name="returned_gradients",
    )(owners, came)


def pull_kernel(place_ref, free_own_ref, free_other_ref, sums_ref, pooled_ref, labels_ref, pulled_ref, *outs):
    free = jnp.concatenate([free_own_ref[...], free_other_ref[...]], axis=0)
    sums = sums_ref[...]
    unit = unit_rows(sums)
    along = jnp.sum(sums * free, axis=-1, keepdims=True)
    pulled = unit * free - (unit * unit * unit * along) * sums
    pulled_ref[...] = pulled
    for f in range(N_Z):
        acts = pooled_ref[lax.rem(place_ref[4] + f, N_Z)]
        for k in range(FACTOR_ROWS // (2 * TXT)):
            piece = acts[:, k * 128 : (k + 1) * 128] if k < 2 else pulled[:, (k - 2) * 128 : (k - 1) * 128]
            outs[f][k * 2 * TXT : (k + 1) * 2 * TXT] = piece
        outs[f][FACTOR_ROWS:] = labels_ref[...]


def pull(place, free_own, free_other, sums, pooled, label_rows):
    return pl.pallas_call(
        pull_kernel,
        out_shape=(jax.ShapeDtypeStruct((2 * TXT, HALF), f32),)
        + (jax.ShapeDtypeStruct((MOVED_ROWS, 128), f32),) * N_Z,
        in_specs=smem(1) + vmem(5),
        out_specs=tuple(vmem(1 + N_Z)),
        compiler_params=params(12),
        cost_estimate=cost(6 * 32 * HALF * D, 3 * 10**6),
        name="pull_back",
    )(place, free_own, free_other, sums, pooled, label_rows)


def w_out_kernel(pulled_ref, high_ref, low_ref, back_ref):
    p_high, p_low = split(pulled_ref[...])
    back_ref[...] = jnp.concatenate(
        [
            dot(p_high, high_ref[z], NT) + (dot(p_high, low_ref[z], NT) + dot(p_low, high_ref[z], NT))
            for z in range(N_Z)
        ],
        axis=1,
    )


def through_w_out(pulled, high, low):
    return pl.pallas_call(
        w_out_kernel,
        out_shape=jax.ShapeDtypeStruct((2 * TXT, HALF), f32),
        in_specs=vmem(3),
        out_specs=pl.BlockSpec(memory_space=pltpu.VMEM),
        compiler_params=params(12),
        cost_estimate=cost(6 * 32 * HALF * D, 3 * 10**6),
        name="back_through_w_out",
    )(pulled, high, low)


def backward_kernel(back_ref, gain_ref, own_ref, other_ref, slope_ref, grad, largest, x_buf, slope_buf, sem):
    copies = []
    for q in range(PARTS):
        x_rows = slice(q % (PARTS // 2) * PART, (q % (PARTS // 2) + 1) * PART)
        x_ref = (own_ref, other_ref)[q // (PARTS // 2)]
        rows = slice(q * PART, (q + 1) * PART)
        copies.append(
            (
                pltpu.make_async_copy(x_ref.at[x_rows], x_buf.at[q], sem.at[0, q]),
                pltpu.make_async_copy(slope_ref.at[rows], slope_buf.at[q], sem.at[1, q]),
            )
        )
    for copy in copies[0]:
        copy.start()
    for q in range(PARTS):
        for copy in copies[q]:
            copy.wait()
        if q + 1 < PARTS:
            for copy in copies[q + 1]:
                copy.start()

        def product(j):
            cols = slice(j * 256, (j + 1) * 256)
            total = jnp.zeros((256, D), f32)
            for i in range(PART // TOKENS):
                pieces = []
                for t in range(i * TEXTS_STEP, (i + 1) * TEXTS_STEP):
                    text = q * (PART // LMAX) + t
                    pieces.append(slope_buf[q, t * LMAX : (t + 1) * LMAX, cols] * back_ref[text : text + 1, cols])
                high, low = split(jnp.concatenate(pieces, axis=0))
                x = x_buf[q, i * TOKENS : (i + 1) * TOKENS]
                total = total + (dot(high, x, TN) + dot(low, x, TN))
            if q > 0:
                total = total + grad[cols]
            if q == PARTS - 1:
                total = total * gain_ref[...]
                largest[j : j + 1] = jnp.max(jnp.abs(total), axis=0, keepdims=True)
            grad[cols] = total

        for j in range(HALF // 256):
            product(j)


def backward(back, gain, own, other, slope):
    tokens = 2 * TXT * LMAX
    shape = jax.ShapeDtypeStruct
    return pl.pallas_call(
        backward_kernel,
        out_shape=(shape((HALF, D), f32), shape((HALF // 256, D), f32)),
        in_specs=vmem(2) + [HBM] * 3,
        out_specs=tuple(vmem(2)),
        scratch_shapes=[
            pltpu.VMEM((PARTS, PART, D), bf16),
            pltpu.VMEM((PARTS, PART, HALF), f32),
            pltpu.SemaphoreType.DMA((2, PARTS)),
        ],
        compiler_params=params(24),
        cost_estimate=cost(5 * tokens * HALF * D, 4 * 10**6),
        name="encoder_backward",
    )(back, gain, in_hbm(own), in_hbm(other), in_hbm(slope))


def power_of(top):
    return jnp.clip(jnp.floor(14.0 - jnp.log2(jnp.maximum(top, 1e-30))), -100.0, 100.0)


def finish_kernel(grad_ref, largest_ref, *rest):
    factors, out_ref = rest[:N_Z], rest[N_Z]
    wide = jnp.concatenate(
        [
            jnp.concatenate([ref[k * 2 * TXT : (k + 1) * 2 * TXT] for ref in factors], axis=0)
            for k in range(FACTOR_ROWS // (2 * TXT))
        ],
        axis=1,
    )
    block = dot3(wide[:, :BLOCK], wide[:, 256:], TN)
    top = jnp.max(jnp.max(largest_ref[...], axis=0, keepdims=True), axis=1, keepdims=True)
    block_top = jnp.max(jnp.max(jnp.abs(block), axis=0, keepdims=True), axis=1, keepdims=True)
    power, block_power = power_of(top), power_of(block_top)
    scale = jnp.exp2(power)
    block = block * jnp.exp2(block_power)
    powers = jnp.where(iota((8, 128), 0) < 4, power, block_power)
    for lab in range(N_LABEL):
        first = lab * SENT_ROWS
        for j in range(PIECES):
            start = first + AT_W_OUT + j * ROWS
            out_ref[start : start + ROWS] = block[lab * ROWS : (lab + 1) * ROWS, j * 128 : (j + 1) * 128]
        out_ref[first + AT_POWERS : first + AT_LABELS] = powers
    for f in range(N_Z):
        for g in range(N_LABEL // 8):
            for k in range(SLOT_ROWS):
                start = g * 8 * SENT_ROWS + AT_LABELS + f * SLOT_ROWS + k
                row = FACTOR_ROWS + (g * SLOT_ROWS + k) * 8
                out_ref[pl.ds(start, 8, stride=SENT_ROWS)] = factors[f][row : row + 8]
    for z in range(N_Z):
        for k in range(N_LABEL // 2):
            start = z * BLOCK + k * 2 * ROWS
            rows = grad_ref[start : start + 2 * ROWS] * scale
            for g in range(2):
                for j in range(PIECES):
                    piece = rows[g * ROWS : (g + 1) * ROWS, j * 128 : (j + 1) * 128]
                    first = (2 * k + g) * SENT_ROWS + z * CHUNK + j * ROWS
                    out_ref[first : first + ROWS] = piece


def finish(grad, largest, factors):
    return pl.pallas_call(
        finish_kernel,
        out_shape=jax.ShapeDtypeStruct((N_LABEL * SENT_ROWS, 128), f32),
        in_specs=vmem(2 + N_Z),
        out_specs=pl.BlockSpec(memory_space=pltpu.VMEM),
        compiler_params=params(16),
        cost_estimate=cost(10**9, 5 * 10**6),
        name="finish_gradients",
    )(grad, largest, *factors)


def unpieced(rows):
    return jnp.concatenate([rows[j * ROWS : (j + 1) * ROWS] for j in range(PIECES)], axis=1)


def middle_kernel(place_ref, came_ref, w_out_ref, table_ref, *outs):
    total = jnp.zeros((AT_W_OUT, 128), f32)
    block = jnp.zeros((CHUNK, 128), f32)
    for lab in range(N_LABEL):
        total = total + came_ref[lab, :AT_W_OUT] * jnp.exp2(-came_ref[lab, AT_POWERS : AT_POWERS + 1])
        block = block + came_ref[lab, AT_W_OUT:AT_POWERS] * jnp.exp2(-came_ref[lab, AT_POWERS + 4 : AT_POWERS + 5])
    w_out_ref[...] = unpieced(block)
    for f in range(N_Z):
        z = lax.rem(place_ref[4] - f + N_Z, N_Z)
        for lab in range(N_LABEL):
            first = AT_LABELS + f * SLOT_ROWS
            table_ref[z, lab * SLOT_ROWS : (lab + 1) * SLOT_ROWS] = came_ref[lab, first : first + SLOT_ROWS] * (
                1.0 / LABEL_SCALE
            )
    for z in range(N_Z):
        for f in range(N_Z):

            @pl.when(lax.rem(place_ref[4] + f, N_Z) == z)
            def _(z=z, f=f):
                outs[f][...] = total[z * CHUNK : (z + 1) * CHUNK]


def middle(place, came):
    return pl.pallas_call(
        middle_kernel,
        out_shape=(
            jax.ShapeDtypeStruct((ROWS, D), f32),
            jax.ShapeDtypeStruct((N_Z, N_LABEL * SLOT_ROWS, 128), f32),
        )
        + (jax.ShapeDtypeStruct((CHUNK, 128), f32),) * N_Z,
        in_specs=smem(1) + vmem(1),
        out_specs=tuple(vmem(2 + N_Z)),
        compiler_params=params(16),
        cost_estimate=cost(10**7, 4 * 10**6),
        name="plane_sums",
    )(place, came)


def last_kernel(*rest):
    blocks, w_in_ref = rest[:N_Z], rest[-1]
    w_in_ref[...] = unpieced((blocks[0][...] + blocks[1][...]) + (blocks[2][...] + blocks[3][...]))


def last(blocks, after):
    return pl.pallas_call(
        last_kernel,
        out_shape=jax.ShapeDtypeStruct((ROWS, D), f32),
        in_specs=vmem(N_Z) + [HBM],
        out_specs=pl.BlockSpec(memory_space=pltpu.VMEM),
        compiler_params=params(8),
        cost_estimate=cost(10**6, 10**6),
        name="z_sums",
    )(*blocks, in_hbm(after))


def swap(value):
    return lax.ppermute(value, "core", ((0, 1), (1, 0)))


def shift(blocks, axis):
    moved = [lax.ppermute(blocks[k], axis, [(i, (i + k) % 4) for i in range(4)]) for k in range(1, 4)]
    return [blocks[0]] + moved


def exchange(value, axes):
    return lax.all_to_all(value, axes, split_axis=0, concat_axis=0, tiled=True)


def local(texts, lengths, owners, gain, w_in, w_out, free_vectors, queries, shortlist, grad_scores):
    core, x, y, z = (lax.axis_index(name) for name in ("core", "x", "y", "z"))
    place = jnp.stack([core, x * N_Y + y, x, y, z]).astype(jnp.int32)
    own = texts.reshape(TXT * LMAX, D)
    other = swap(own)
    both_lengths = jnp.concatenate([lengths, swap(lengths)])
    owner_ids = owners[:, 0]
    names = shortlist.T
    gain_row = gain.reshape(1, D)
    w_in_blocks = w_in.reshape(N_Z, N_CORE, BLOCK, D)
    w_out_blocks = w_out.reshape(N_Z, N_CORE, BLOCK, D)

    kept, sent = slot_partials(place, names, grad_scores, queries)
    slots = exchange((kept + swap(sent)).reshape(N_CHIPS, 16, 128), ("z", "x", "y"))

    slope, pooled, part, high, low = forward(place, both_lengths, gain_row, own, other, w_in_blocks, w_out_blocks)
    sums, label_rows = labels(owner_ids, part, swap(part), free_vectors)

    free_grad, free_own = returned(owner_ids, slots)
    pulled, *factors = pull(place, free_own, swap(free_own), sums, pooled, label_rows)
    back = through_w_out(pulled, high, low)
    factors = shift(factors, "z")
    grad, largest = backward(back, gain_row, own, other, slope)
    sent_rows = finish(grad, largest, factors).reshape(N_LABEL, SENT_ROWS, 128)
    came = exchange(sent_rows.astype(jnp.float16), LABEL).astype(f32)
    w_out_grad, table, *moved = middle(place, came)
    table = table.reshape(N_CHIPS * SLOT_ROWS, 128)
    moved = shift(moved, "z")
    scores = slot_scores(place, names, queries, table, swap(table))
    w_in_grad = last(moved, scores)
    return scores, free_grad, w_in_grad, w_out_grad


def solution(mesh):
    fine = Mesh(mesh.devices.reshape(N_Z, N_CORE, N_X, N_Y), ("z", "core", "x", "y"))
    dp, every = ("z", "core"), ("z", "core", "x", "y")
    placed = (
        P(every, None, None),
        P(every),
        P(every, None),
        P(),
        P(),
        P(),
        P(every, None),
        P(dp, None),
        P(dp, None),
        P(dp, LABEL),
    )
    return jax.shard_map(
        local,
        mesh=fine,
        in_specs=placed,
        out_specs=(
            P(dp, LABEL),
            P(every, None),
            P(every, None),
            P(every, None),
        ),
        check_vma=False,
    )
```

```python
import functools
import math

import jax
import jax.numpy as jnp
from jax import lax
from jax.experimental import pallas as pl
from jax.experimental.pallas import tpu as pltpu
from jax.sharding import Mesh, PartitionSpec as P

N_Z, N_CORE, N_X, N_Y = 4, 2, 4, 4
N_LABEL = N_X * N_Y
TXT = 16
LMAX = 64
D = 768
FF = 1536
HALF = FF // 2
BLOCK = FF // (N_Z * N_CORE)
ROWS = BLOCK // N_LABEL
CAP = 2
SLOTS = N_LABEL * CAP
QROWS = 512
TOKENS = 256
TEXTS_STEP = TOKENS // LMAX
STEPS = 2 * TXT // TEXTS_STEP
C0 = math.sqrt(2.0 / math.pi)
C1 = C0 * 0.044715
MIB = 1024 * 1024

f32 = jnp.float32
bf16 = jnp.bfloat16
N_CHIPS = N_Z * N_LABEL
CHIP_SLOTS = N_CHIPS * CAP
PIECES = D // 128
CHUNK = PIECES * ROWS
SLOT_ROWS = CAP * PIECES
CHIP_ROWS = N_CORE * SLOT_ROWS
AT_W_OUT = N_Z * CHUNK
AT_POWERS = AT_W_OUT + CHUNK
AT_LABELS = AT_POWERS + 8
SENT_ROWS = AT_LABELS + N_Z * SLOT_ROWS
FACTOR_ROWS = 2 * TXT * (256 + D) // 128
MOVED_ROWS = FACTOR_ROWS + N_LABEL * SLOT_ROWS
LABEL_SCALE = 256.0
PARTS = 2
PART = 2 * TXT * LMAX // PARTS
LABEL = ("x", "y")


def split(value):
    high = value.astype(bf16)
    return high, (value - high.astype(f32)).astype(bf16)


def dot(a, b, dims):
    return lax.dot_general(a, b, (dims, ((), ())), preferred_element_type=f32)


def dot3(a, b, dims):
    a_high, a_low = split(a)
    b_high, b_low = split(b)
    return dot(a_high, b_high, dims) + (dot(a_high, b_low, dims) + dot(a_low, b_high, dims))


def params(mib):
    return pltpu.CompilerParams(vmem_limit_bytes=mib * MIB)


def vmem(count):
    return [pl.BlockSpec(memory_space=pltpu.VMEM)] * count


def smem(count):
    return [pl.BlockSpec(memory_space=pltpu.SMEM)] * count


def is_kept(shortlist_ref, label):
    row = jnp.max((shortlist_ref[...] == label).astype(f32), axis=0, keepdims=True)
    return jnp.broadcast_to(row, (8, QROWS)).T[:, :1]


def iota(shape, axis):
    return lax.broadcasted_iota(jnp.int32, shape, axis)


def in_hbm(value):
    return pltpu.with_memory_space_constraint(value, pltpu.HBM)


def cost(flops, nbytes):
    return pl.CostEstimate(flops=flops, bytes_accessed=nbytes, transcendentals=0)


ANY = pl.BlockSpec(memory_space=pl.ANY)
HBM = pl.BlockSpec(memory_space=pltpu.HBM)
NN, NT, TN = ((1,), (0,)), ((1,), (1,)), ((0,), (0,))


def partial_kernel(place_ref, shortlist_ref, grad_ref, queries_ref, out_ref):
    weighted = grad_ref[...] * is_kept(shortlist_ref, place_ref[1])
    size = 2 * CHIP_SLOTS
    target = iota((size, size), 1)
    core = target // CHIP_SLOTS
    rank = target // N_CHIPS % CAP
    z = target // N_LABEL % N_Z
    lab = target % N_LABEL
    source = ((z * N_CORE + core) * N_LABEL + lab) * CAP + rank
    order = (iota((size, size), 0) == source).astype(bf16)
    w_high, w_low = (dot(part, order, NN).astype(bf16) for part in split(weighted))
    q_high, q_low = split(queries_ref[...])
    total = dot(w_high, q_high, TN) + (dot(w_high, q_low, TN) + dot(w_low, q_high, TN))
    for k in range(N_CORE * CAP):
        start = k * N_CHIPS
        for j in range(PIECES):
            out_ref[pl.ds(PIECES * k + j, N_CHIPS, stride=CHIP_ROWS)] = total[
                start : start + N_CHIPS, j * 128 : (j + 1) * 128
            ]


def slot_partials(place, shortlist, grad_scores, queries):
    return pl.pallas_call(
        partial_kernel,
        out_shape=jax.ShapeDtypeStruct((N_CHIPS * CHIP_ROWS, 128), f32),
        in_specs=smem(1) + vmem(3),
        out_specs=pl.BlockSpec(memory_space=pltpu.VMEM),
        compiler_params=params(24),
        cost_estimate=cost(6 * QROWS * 256 * D, 4 * 10**6),
        name="slot_partials",
    )(place, in_hbm(shortlist), in_hbm(grad_scores), in_hbm(queries))


def forward_kernel(
    place_ref,
    lengths_ref,
    gain_ref,
    own_ref,
    other_ref,
    w_in_ref,
    w_out_ref,
    slope_ref,
    pooled_ref,
    sums_ref,
    out_high_ref,
    out_low_ref,
    w_in_buf,
    w_out_buf,
    x_buf,
    slope_even,
    slope_odd,
    keep_even,
    keep_odd,
    w_high,
    w_low,
    pooled,
    pooled_x,
    w_sem,
    x_sem,
    slope_sem,
):
    core = place_ref[0]
    w_copies = [
        pltpu.make_async_copy(ref.at[:, core], buf, w_sem.at[i])
        for i, (ref, buf) in enumerate(((w_in_ref, w_in_buf), (w_out_ref, w_out_buf)))
    ]
    x_copies = [pltpu.make_async_copy(ref, x_buf.at[i], x_sem.at[i]) for i, ref in enumerate((own_ref, other_ref))]
    w_copies[0].start()
    x_copies[0].start()
    w_copies[0].wait()
    x_copies[1].start()
    w_copies[1].start()
    for z in range(N_Z):
        rows = slice(z * BLOCK, (z + 1) * BLOCK)
        w_high[rows], w_low[rows] = split(w_in_buf[z] * gain_ref[...])
    position = iota((LMAX, 1), 0)

    keeps, slope_bufs = (keep_even, keep_odd), (slope_even, slope_odd)

    def store_from(buf, parity, step):
        rows = slice(step * TOKENS, (step + 1) * TOKENS)
        return pltpu.make_async_copy(buf, slope_ref.at[rows], slope_sem.at[parity])

    def tokens_of(step):
        start = step % (STEPS // 2) * TOKENS
        return x_buf[step // (STEPS // 2), start : start + TOKENS]

    def product(step, keep):
        x = tokens_of(step)
        for j in range(HALF // 256):
            cols = slice(j * 256, (j + 1) * 256)
            keep[:, cols] = dot(x, w_high[cols], NT) + dot(x, w_low[cols], NT)

    def turn(step, now, later, slope_out, copy):
        if step >= 2:
            copy(step - 2).wait()
        if step + 1 < STEPS:
            product(step + 1, later)
        xf = tokens_of(step).astype(f32)
        inverse = lax.rsqrt(jnp.sum(xf * xf, axis=1, keepdims=True) * (1.0 / D) + 1e-05)
        weights = []
        for i in range(TEXTS_STEP):
            length = lengths_ref[step * TEXTS_STEP + i]
            scale = 1.0 / jnp.full((1, 1), length, jnp.int32).astype(f32)
            weights.append(jnp.where(position < length, scale, 0.0))
            rows = slice(i * LMAX, (i + 1) * LMAX)
            pooled_x[step, i : i + 1] = jnp.sum(xf[rows] * weights[i], axis=0, keepdims=True)
        weight = jnp.concatenate(weights, axis=0)
        scaled = weight * inverse
        for j in range(HALF // 256):
            cols = slice(j * 256, (j + 1) * 256)
            p = now[:, cols] * inverse
            p2 = p * p
            half = 0.5 + 0.5 * jnp.tanh(p * (C0 + C1 * p2))
            act = p * half
            slope = half + (act - act * half) * (2.0 * C0 + 6.0 * C1 * p2)
            slope_out[:, cols] = slope * scaled
            act = act * weight
            for i in range(TEXTS_STEP):
                rows = slice(i * LMAX, (i + 1) * LMAX)
                pooled[step, i : i + 1, cols] = jnp.sum(act[rows], axis=0, keepdims=True)
        copy(step).start()

    x_copies[0].wait()
    product(0, keeps[0])
    for step in range(STEPS):
        if step == STEPS // 2 - 1:
            x_copies[1].wait()
        parity = step % 2
        store = functools.partial(store_from, slope_bufs[parity], parity)
        turn(step, keeps[parity], keeps[1 - parity], slope_bufs[parity], store)
    w_copies[1].wait()
    acts = jnp.concatenate([pooled[i] for i in range(STEPS)], axis=0)
    total = 0.5 * jnp.concatenate([pooled_x[i] for i in range(STEPS)], axis=0)
    for z in range(N_Z):
        high, low = split(w_out_buf[z])
        out_high_ref[z] = high
        out_low_ref[z] = low
        a = acts[:, z * BLOCK : (z + 1) * BLOCK]
        pooled_ref[z] = jnp.concatenate([a, jnp.zeros((2 * TXT, 256 - BLOCK), f32)], axis=1)
        a_high, a_low = split(a)
        total = total + (dot(a_high, high, NN) + (dot(a_high, low, NN) + dot(a_low, high, NN)))
    sums_ref[...] = total
    for parity in range(2):
        store_from(slope_bufs[parity], parity, STEPS - 2 + parity).wait()


def forward(place, lengths, gain, own, other, w_in, w_out):
    tokens = 2 * TXT * LMAX
    shape = jax.ShapeDtypeStruct
    return pl.pallas_call(
        forward_kernel,
        out_shape=(
            pltpu.HBM((tokens, HALF), f32),
            shape((N_Z, 2 * TXT, 256), f32),
            shape((2 * TXT, D), f32),
            shape((N_Z, BLOCK, D), bf16),
            shape((N_Z, BLOCK, D), bf16),
        ),
        in_specs=smem(2) + vmem(1) + [HBM] * 4,
        out_specs=(HBM, *vmem(4)),
        scratch_shapes=[
            pltpu.VMEM((N_Z, BLOCK, D), f32),
            pltpu.VMEM((N_Z, BLOCK, D), f32),
            pltpu.VMEM((2, TXT * LMAX, D), bf16),
            pltpu.VMEM((TOKENS, HALF), f32),
            pltpu.VMEM((TOKENS, HALF), f32),
            pltpu.VMEM((TOKENS, HALF), f32),
            pltpu.VMEM((TOKENS, HALF), f32),
            pltpu.VMEM((HALF, D), bf16),
            pltpu.VMEM((HALF, D), bf16),
            pltpu.VMEM((STEPS, TEXTS_STEP, HALF), f32),
            pltpu.VMEM((STEPS, TEXTS_STEP, D), f32),
            pltpu.SemaphoreType.DMA((2,)),
            pltpu.SemaphoreType.DMA((2,)),
            pltpu.SemaphoreType.DMA((2,)),
        ],
        compiler_params=params(24),
        cost_estimate=cost(10 * tokens * HALF * D, 8 * 10**6),
        name="encoder_forward",
    )(place, lengths, gain, in_hbm(own), in_hbm(other), in_hbm(w_in), in_hbm(w_out))


def unit_rows(sums):
    return lax.rsqrt(jnp.sum(sums * sums, axis=-1, keepdims=True) + 1e-06)


def each_label(owners_ref, counts, put, first=0):
    for o in range(N_LABEL):
        counts[o] = 0
    for i in range(TXT):
        owner = owners_ref[first + i]
        rank = counts[owner]
        counts[owner] = rank + 1
        put(i, owner, jnp.minimum(rank, CAP - 1))


def label_kernel(owners_ref, part_ref, came_ref, free_ref, sums_ref, out_ref, counts):
    own = part_ref[:TXT] + came_ref[TXT:]
    sums_ref[:TXT] = own
    sums_ref[TXT:] = part_ref[TXT:] + came_ref[:TXT]
    scaled = (own * unit_rows(own) + free_ref[...]) * LABEL_SCALE
    out_ref[...] = jnp.zeros_like(out_ref)

    def put(i, owner, rank):
        first = owner // 8 * (8 * SLOT_ROWS) + rank * (8 * PIECES) + lax.rem(owner, 8)
        for j in range(PIECES):
            out_ref[pl.ds(first + 8 * j, 1)] = scaled[i : i + 1, j * 128 : (j + 1) * 128]

    each_label(owners_ref, counts, put)


def labels(owners, part, came, free_vectors):
    return pl.pallas_call(
        label_kernel,
        out_shape=(
            jax.ShapeDtypeStruct((2 * TXT, D), f32),
            jax.ShapeDtypeStruct((N_LABEL * SLOT_ROWS, 128), f32),
        ),
        in_specs=smem(1) + vmem(3),
        out_specs=tuple(vmem(2)),
        scratch_shapes=[pltpu.SMEM((N_LABEL,), jnp.int32)],
        compiler_params=params(8),
        cost_estimate=cost(10**6, 8 * 10**5),
        name="label_vectors",
    )(owners, part, came, free_vectors)


def scores_kernel(place_ref, shortlist_ref, queries_ref, own_ref, other_ref, out_ref):
    size = 2 * CHIP_SLOTS
    column = iota((size, size), 0)
    rank = column % CAP
    lab = column // CAP % N_LABEL
    core = column // (CAP * N_LABEL) % N_CORE
    z = column // (CAP * N_LABEL * N_CORE)
    half = jnp.where(core == place_ref[0], 0, 1)
    source = half * CHIP_SLOTS + rank * N_CHIPS + z * N_LABEL + lab
    order = (iota((size, size), 1) == source).astype(bf16)
    table = jnp.concatenate(
        [
            jnp.concatenate(
                [ref[pl.ds(PIECES * r + j, N_CHIPS, stride=SLOT_ROWS)] for j in range(PIECES)],
                axis=1,
            )
            for ref in (own_ref, other_ref)
            for r in range(CAP)
        ],
        axis=0,
    )
    t_high, t_low = (dot(order, part, NN).astype(bf16) for part in split(table))
    q_high, q_low = split(queries_ref[...])
    scores = dot(q_high, t_high, NT) + (dot(q_high, t_low, NT) + dot(q_low, t_high, NT))
    out_ref[...] = scores * is_kept(shortlist_ref, place_ref[1])


def slot_scores(place, shortlist, queries, own, other):
    return pl.pallas_call(
        scores_kernel,
        out_shape=jax.ShapeDtypeStruct((QROWS, 2 * CHIP_SLOTS), f32),
        in_specs=smem(1) + vmem(4),
        out_specs=pl.BlockSpec(memory_space=pltpu.VMEM),
        compiler_params=params(24),
        cost_estimate=cost(6 * QROWS * 256 * D, 4 * 10**6),
        name="slot_scores",
    )(place, shortlist, queries, own, other)


def return_kernel(place_ref, owners_ref, came_ref, out_ref, counts):
    for h in range(N_CORE):
        core = place_ref[0] if h == 0 else 1 - place_ref[0]

        def put(i, owner, rank, h=h, core=core):
            value = came_ref[owner]
            for z in range(1, N_Z):
                value = value + came_ref[z * N_LABEL + owner]
            value = jnp.where(core == 0, value[:SLOT_ROWS], value[SLOT_ROWS:])
            value = jnp.where(rank == 0, value[:PIECES], value[PIECES:])
            row = h * TXT + i
            for j in range(PIECES):
                out_ref[row : row + 1, j * 128 : (j + 1) * 128] = value[j : j + 1]

        each_label(owners_ref, counts, put, h * TXT)


def returned(place, owners, came):
    return pl.pallas_call(
        return_kernel,
        out_shape=jax.ShapeDtypeStruct((2 * TXT, D), f32),
        in_specs=smem(2) + vmem(1),
        out_specs=pl.BlockSpec(memory_space=pltpu.VMEM),
        scratch_shapes=[pltpu.SMEM((N_LABEL,), jnp.int32)],
        compiler_params=params(8),
        cost_estimate=cost(10**5, 5 * 10**5),
        name="returned_gradients",
    )(place, owners, came)


def pull_kernel(place_ref, free_ref, came_ref, sums_ref, pooled_ref, labels_ref, pulled_ref, free_grad_ref, *outs):
    own = free_ref[:TXT] + came_ref[TXT:]
    free_grad_ref[...] = own
    free = jnp.concatenate([own, free_ref[TXT:] + came_ref[:TXT]], axis=0)
    sums = sums_ref[...]
    unit = unit_rows(sums)
    along = jnp.sum(sums * free, axis=-1, keepdims=True)
    pulled = unit * free - (unit * unit * unit * along) * sums
    pulled_ref[...] = pulled
    for f in range(N_Z):
        acts = pooled_ref[lax.rem(place_ref[4] + f, N_Z)]
        for k in range(FACTOR_ROWS // (2 * TXT)):
            piece = acts[:, k * 128 : (k + 1) * 128] if k < 2 else pulled[:, (k - 2) * 128 : (k - 1) * 128]
            outs[f][k * 2 * TXT : (k + 1) * 2 * TXT] = piece
        outs[f][FACTOR_ROWS:] = labels_ref[...]


def pull(place, free, came, sums, pooled, label_rows):
    return pl.pallas_call(
        pull_kernel,
        out_shape=(jax.ShapeDtypeStruct((2 * TXT, D), f32), jax.ShapeDtypeStruct((TXT, D), f32))
        + (jax.ShapeDtypeStruct((MOVED_ROWS, 128), f32),) * N_Z,
        in_specs=smem(1) + vmem(5),
        out_specs=tuple(vmem(2 + N_Z)),
        compiler_params=params(12),
        cost_estimate=cost(6 * 32 * HALF * D, 3 * 10**6),
        name="pull_back",
    )(place, free, came, sums, pooled, label_rows)


def w_out_kernel(pulled_ref, high_ref, low_ref, back_ref):
    p_high, p_low = split(pulled_ref[...])
    back_ref[...] = jnp.concatenate(
        [
            dot(p_high, high_ref[z], NT) + (dot(p_high, low_ref[z], NT) + dot(p_low, high_ref[z], NT))
            for z in range(N_Z)
        ],
        axis=1,
    )


def through_w_out(pulled, high, low):
    return pl.pallas_call(
        w_out_kernel,
        out_shape=jax.ShapeDtypeStruct((2 * TXT, HALF), f32),
        in_specs=vmem(3),
        out_specs=pl.BlockSpec(memory_space=pltpu.VMEM),
        compiler_params=params(12),
        cost_estimate=cost(6 * 32 * HALF * D, 3 * 10**6),
        name="back_through_w_out",
    )(pulled, high, low)


def backward_kernel(back_ref, gain_ref, own_ref, other_ref, slope_ref, grad, largest, x_buf, slope_buf, sem):
    copies = []
    for q in range(PARTS):
        x_rows = slice(q % (PARTS // 2) * PART, (q % (PARTS // 2) + 1) * PART)
        x_ref = (own_ref, other_ref)[q // (PARTS // 2)]
        rows = slice(q * PART, (q + 1) * PART)
        copies.append(
            (
                pltpu.make_async_copy(x_ref.at[x_rows], x_buf.at[q], sem.at[0, q]),
                pltpu.make_async_copy(slope_ref.at[rows], slope_buf.at[q], sem.at[1, q]),
            )
        )
    for copy in copies[0]:
        copy.start()
    for q in range(PARTS):
        for copy in copies[q]:
            copy.wait()
        if q + 1 < PARTS:
            for copy in copies[q + 1]:
                copy.start()

        def product(j):
            cols = slice(j * 256, (j + 1) * 256)
            total = jnp.zeros((256, D), f32)
            for i in range(PART // TOKENS):
                pieces = []
                for t in range(i * TEXTS_STEP, (i + 1) * TEXTS_STEP):
                    text = q * (PART // LMAX) + t
                    pieces.append(slope_buf[q, t * LMAX : (t + 1) * LMAX, cols] * back_ref[text : text + 1, cols])
                high, low = split(jnp.concatenate(pieces, axis=0))
                x = x_buf[q, i * TOKENS : (i + 1) * TOKENS]
                total = total + (dot(high, x, TN) + dot(low, x, TN))
            if q > 0:
                total = total + grad[cols]
            if q == PARTS - 1:
                total = total * gain_ref[...]
                largest[j : j + 1] = jnp.max(jnp.abs(total), axis=0, keepdims=True)
            grad[cols] = total

        for j in range(HALF // 256):
            product(j)


def backward(back, gain, own, other, slope):
    tokens = 2 * TXT * LMAX
    shape = jax.ShapeDtypeStruct
    return pl.pallas_call(
        backward_kernel,
        out_shape=(shape((HALF, D), f32), shape((HALF // 256, D), f32)),
        in_specs=vmem(2) + [HBM] * 3,
        out_specs=tuple(vmem(2)),
        scratch_shapes=[
            pltpu.VMEM((PARTS, PART, D), bf16),
            pltpu.VMEM((PARTS, PART, HALF), f32),
            pltpu.SemaphoreType.DMA((2, PARTS)),
        ],
        compiler_params=params(24),
        cost_estimate=cost(5 * tokens * HALF * D, 4 * 10**6),
        name="encoder_backward",
    )(back, gain, in_hbm(own), in_hbm(other), in_hbm(slope))


def power_of(top):
    return jnp.clip(jnp.floor(14.0 - jnp.log2(jnp.maximum(top, 1e-30))), -100.0, 100.0)


def finish_kernel(grad_ref, largest_ref, *rest):
    factors, out_ref = rest[:N_Z], rest[N_Z]
    wide = jnp.concatenate(
        [
            jnp.concatenate([ref[k * 2 * TXT : (k + 1) * 2 * TXT] for ref in factors], axis=0)
            for k in range(FACTOR_ROWS // (2 * TXT))
        ],
        axis=1,
    )
    block = dot3(wide[:, :BLOCK], wide[:, 256:], TN)
    top = jnp.max(jnp.max(largest_ref[...], axis=0, keepdims=True), axis=1, keepdims=True)
    block_top = jnp.max(jnp.max(jnp.abs(block), axis=0, keepdims=True), axis=1, keepdims=True)
    power, block_power = power_of(top), power_of(block_top)
    scale = jnp.exp2(power)
    block = block * jnp.exp2(block_power)
    powers = jnp.where(iota((8, 128), 0) < 4, power, block_power)
    for lab in range(N_LABEL):
        first = lab * SENT_ROWS
        for j in range(PIECES):
            start = first + AT_W_OUT + j * ROWS
            out_ref[start : start + ROWS] = block[lab * ROWS : (lab + 1) * ROWS, j * 128 : (j + 1) * 128]
        out_ref[first + AT_POWERS : first + AT_LABELS] = powers
    for f in range(N_Z):
        for g in range(N_LABEL // 8):
            for k in range(SLOT_ROWS):
                start = g * 8 * SENT_ROWS + AT_LABELS + f * SLOT_ROWS + k
                row = FACTOR_ROWS + (g * SLOT_ROWS + k) * 8
                out_ref[pl.ds(start, 8, stride=SENT_ROWS)] = factors[f][row : row + 8]
    for z in range(N_Z):
        for k in range(N_LABEL // 2):
            start = z * BLOCK + k * 2 * ROWS
            rows = grad_ref[start : start + 2 * ROWS] * scale
            for g in range(2):
                for j in range(PIECES):
                    piece = rows[g * ROWS : (g + 1) * ROWS, j * 128 : (j + 1) * 128]
                    first = (2 * k + g) * SENT_ROWS + z * CHUNK + j * ROWS
                    out_ref[first : first + ROWS] = piece


def finish(grad, largest, factors):
    return pl.pallas_call(
        finish_kernel,
        out_shape=jax.ShapeDtypeStruct((N_LABEL * SENT_ROWS, 128), f32),
        in_specs=vmem(2 + N_Z),
        out_specs=pl.BlockSpec(memory_space=pltpu.VMEM),
        compiler_params=params(16),
        cost_estimate=cost(10**9, 5 * 10**6),
        name="finish_gradients",
    )(grad, largest, *factors)


def unpieced(rows):
    return jnp.concatenate([rows[j * ROWS : (j + 1) * ROWS] for j in range(PIECES)], axis=1)


def middle_kernel(place_ref, came_ref, w_out_ref, table_ref, *outs):
    total = jnp.zeros((AT_W_OUT, 128), f32)
    block = jnp.zeros((CHUNK, 128), f32)
    for lab in range(N_LABEL):
        total = total + came_ref[lab, :AT_W_OUT] * jnp.exp2(-came_ref[lab, AT_POWERS : AT_POWERS + 1])
        block = block + came_ref[lab, AT_W_OUT:AT_POWERS] * jnp.exp2(-came_ref[lab, AT_POWERS + 4 : AT_POWERS + 5])
    w_out_ref[...] = unpieced(block)
    for f in range(N_Z):
        z = lax.rem(place_ref[4] - f + N_Z, N_Z)
        for lab in range(N_LABEL):
            first = AT_LABELS + f * SLOT_ROWS
            table_ref[z, lab * SLOT_ROWS : (lab + 1) * SLOT_ROWS] = came_ref[lab, first : first + SLOT_ROWS] * (
                1.0 / LABEL_SCALE
            )
    for z in range(N_Z):
        for f in range(N_Z):

            @pl.when(lax.rem(place_ref[4] + f, N_Z) == z)
            def _(z=z, f=f):
                outs[f][...] = total[z * CHUNK : (z + 1) * CHUNK]


def middle(place, came):
    return pl.pallas_call(
        middle_kernel,
        out_shape=(
            jax.ShapeDtypeStruct((ROWS, D), f32),
            jax.ShapeDtypeStruct((N_Z, N_LABEL * SLOT_ROWS, 128), f32),
        )
        + (jax.ShapeDtypeStruct((CHUNK, 128), f32),) * N_Z,
        in_specs=smem(1) + vmem(1),
        out_specs=tuple(vmem(2 + N_Z)),
        compiler_params=params(16),
        cost_estimate=cost(10**7, 4 * 10**6),
        name="plane_sums",
    )(place, came)


def last_kernel(*rest):
    blocks, w_in_ref = rest[:N_Z], rest[-1]
    w_in_ref[...] = unpieced((blocks[0][...] + blocks[1][...]) + (blocks[2][...] + blocks[3][...]))


def last(blocks, after):
    return pl.pallas_call(
        last_kernel,
        out_shape=jax.ShapeDtypeStruct((ROWS, D), f32),
        in_specs=vmem(N_Z) + [HBM],
        out_specs=pl.BlockSpec(memory_space=pltpu.VMEM),
        compiler_params=params(8),
        cost_estimate=cost(10**6, 10**6),
        name="z_sums",
    )(*blocks, in_hbm(after))


def swap(value):
    return lax.ppermute(value, "core", ((0, 1), (1, 0)))


def shift(blocks, axis):
    moved = [lax.ppermute(blocks[k], axis, [(i, (i + k) % 4) for i in range(4)]) for k in range(1, 4)]
    return [blocks[0]] + moved


def exchange(value, axes):
    return lax.all_to_all(value, axes, split_axis=0, concat_axis=0, tiled=True)


def local(texts, lengths, owners, gain, w_in, w_out, free_vectors, queries, shortlist, grad_scores):
    core, x, y, z = (lax.axis_index(name) for name in ("core", "x", "y", "z"))
    place = jnp.stack([core, x * N_Y + y, x, y, z]).astype(jnp.int32)
    own = texts.reshape(TXT * LMAX, D)
    other = swap(own)
    ints = jnp.stack([lengths, owners[:, 0]])
    ints_other = swap(ints)
    both_lengths = jnp.concatenate([ints[0], ints_other[0]])
    owner_ids = jnp.concatenate([ints[1], ints_other[1]])
    names = shortlist.T
    gain_row = gain.reshape(1, D)
    w_in_blocks = w_in.reshape(N_Z, N_CORE, BLOCK, D)
    w_out_blocks = w_out.reshape(N_Z, N_CORE, BLOCK, D)

    slots = slot_partials(place, names, grad_scores, queries).reshape(N_CHIPS, CHIP_ROWS, 128)
    slots = exchange(slots, ("z", "x", "y"))

    slope, pooled, part, high, low = forward(place, both_lengths, gain_row, own, other, w_in_blocks, w_out_blocks)
    sums, label_rows = labels(owner_ids, part, swap(part), free_vectors)

    free = returned(place, owner_ids, slots)
    pulled, free_grad, *factors = pull(place, free, swap(free), sums, pooled, label_rows)
    back = through_w_out(pulled, high, low)
    factors = shift(factors, "z")
    grad, largest = backward(back, gain_row, own, other, slope)
    sent_rows = finish(grad, largest, factors).reshape(N_LABEL, SENT_ROWS, 128)
    came = exchange(sent_rows.astype(jnp.float16), LABEL).astype(f32)
    w_out_grad, table, *moved = middle(place, came)
    table = table.reshape(N_CHIPS * SLOT_ROWS, 128)
    moved = shift(moved, "z")
    scores = slot_scores(place, names, queries, table, swap(table))
    w_in_grad = last(moved, scores)
    return scores, free_grad, w_in_grad, w_out_grad


def solution(mesh):
    fine = Mesh(mesh.devices.reshape(N_Z, N_CORE, N_X, N_Y), ("z", "core", "x", "y"))
    dp, every = ("z", "core"), ("z", "core", "x", "y")
    placed = (
        P(every, None, None),
        P(every),
        P(every, None),
        P(),
        P(),
        P(),
        P(every, None),
        P(dp, None),
        P(dp, None),
        P(dp, LABEL),
    )
    return jax.shard_map(
        local,
        mesh=fine,
        in_specs=placed,
        out_specs=(
            P(dp, LABEL),
            P(every, None),
            P(every, None),
            P(every, None),
        ),
        check_vma=False,
    )
```

```python
import functools
import math

import jax
import jax.numpy as jnp
from jax import lax
from jax.experimental import pallas as pl
from jax.experimental.pallas import tpu as pltpu
from jax.sharding import Mesh, PartitionSpec as P

N_Z, N_CORE, N_X, N_Y = 4, 2, 4, 4
N_LABEL = N_X * N_Y
TXT = 16
LMAX = 64
D = 768
FF = 1536
HALF = FF // 2
BLOCK = FF // (N_Z * N_CORE)
ROWS = BLOCK // N_LABEL
CAP = 2
SLOTS = N_LABEL * CAP
QROWS = 512
TOKENS = 256
TEXTS_STEP = TOKENS // LMAX
STEPS = 2 * TXT // TEXTS_STEP
C0 = math.sqrt(2.0 / math.pi)
C1 = C0 * 0.044715
MIB = 1024 * 1024

f32 = jnp.float32
bf16 = jnp.bfloat16
N_CHIPS = N_Z * N_LABEL
CHIP_SLOTS = N_CHIPS * CAP
PIECES = D // 128
CHUNK = PIECES * ROWS
SLOT_ROWS = CAP * PIECES
CHIP_ROWS = N_CORE * SLOT_ROWS
AT_W_OUT = N_Z * CHUNK
AT_POWERS = AT_W_OUT + CHUNK
AT_LABELS = AT_POWERS + 8
SENT_ROWS = AT_LABELS + N_Z * SLOT_ROWS
FACTOR_ROWS = 2 * TXT * (256 + D) // 128
MOVED_ROWS = FACTOR_ROWS + N_LABEL * SLOT_ROWS
LABEL_SCALE = 256.0
PARTS = 2
PART = 2 * TXT * LMAX // PARTS
LABEL = ("x", "y")


def split(value):
    high = value.astype(bf16)
    return high, (value - high.astype(f32)).astype(bf16)


def dot(a, b, dims):
    return lax.dot_general(a, b, (dims, ((), ())), preferred_element_type=f32)


def dot3(a, b, dims):
    a_high, a_low = split(a)
    b_high, b_low = split(b)
    return dot(a_high, b_high, dims) + (dot(a_high, b_low, dims) + dot(a_low, b_high, dims))


def params(mib):
    return pltpu.CompilerParams(vmem_limit_bytes=mib * MIB)


def vmem(count):
    return [pl.BlockSpec(memory_space=pltpu.VMEM)] * count


def smem(count):
    return [pl.BlockSpec(memory_space=pltpu.SMEM)] * count


def is_kept(shortlist_ref, label):
    row = jnp.max((shortlist_ref[...] == label).astype(f32), axis=0, keepdims=True)
    return jnp.broadcast_to(row, (8, QROWS)).T[:, :1]


def iota(shape, axis):
    return lax.broadcasted_iota(jnp.int32, shape, axis)


def in_hbm(value):
    return pltpu.with_memory_space_constraint(value, pltpu.HBM)


def cost(flops, nbytes):
    return pl.CostEstimate(flops=flops, bytes_accessed=nbytes, transcendentals=0)


ANY = pl.BlockSpec(memory_space=pl.ANY)
HBM = pl.BlockSpec(memory_space=pltpu.HBM)
NN, NT, TN = ((1,), (0,)), ((1,), (1,)), ((0,), (0,))


def partial_kernel(place_ref, shortlist_ref, grad_ref, queries_ref, out_ref):
    weighted = grad_ref[...] * is_kept(shortlist_ref, place_ref[1])
    size = 2 * CHIP_SLOTS
    target = iota((size, size), 1)
    core = target // CHIP_SLOTS
    rank = target // N_CHIPS % CAP
    z = target // N_LABEL % N_Z
    lab = target % N_LABEL
    source = ((z * N_CORE + core) * N_LABEL + lab) * CAP + rank
    order = (iota((size, size), 0) == source).astype(bf16)
    w_high, w_low = (dot(part, order, NN).astype(bf16) for part in split(weighted))
    q_high, q_low = split(queries_ref[...])
    total = dot(w_high, q_high, TN) + (dot(w_high, q_low, TN) + dot(w_low, q_high, TN))
    for k in range(N_CORE * CAP):
        start = k * N_CHIPS
        for j in range(PIECES):
            out_ref[pl.ds(PIECES * k + j, N_CHIPS, stride=CHIP_ROWS)] = total[
                start : start + N_CHIPS, j * 128 : (j + 1) * 128
            ]


def slot_partials(place, shortlist, grad_scores, queries):
    return pl.pallas_call(
        partial_kernel,
        out_shape=jax.ShapeDtypeStruct((N_CHIPS * CHIP_ROWS, 128), f32),
        in_specs=smem(1) + vmem(3),
        out_specs=pl.BlockSpec(memory_space=pltpu.VMEM),
        compiler_params=params(24),
        cost_estimate=cost(6 * QROWS * 256 * D, 4 * 10**6),
        name="slot_partials",
    )(place, in_hbm(shortlist), in_hbm(grad_scores), in_hbm(queries))


def forward_kernel(
    place_ref,
    lengths_ref,
    gain_ref,
    own_ref,
    other_ref,
    w_in_ref,
    w_out_ref,
    slope_ref,
    pooled_ref,
    sums_ref,
    out_high_ref,
    out_low_ref,
    w_in_buf,
    w_out_buf,
    x_buf,
    slope_even,
    slope_odd,
    keep_even,
    keep_odd,
    w_high,
    w_low,
    pooled,
    pooled_x,
    w_sem,
    x_sem,
    slope_sem,
):
    core = place_ref[0]
    w_copies = [
        pltpu.make_async_copy(ref.at[:, core], buf, w_sem.at[i])
        for i, (ref, buf) in enumerate(((w_in_ref, w_in_buf), (w_out_ref, w_out_buf)))
    ]
    x_copies = [pltpu.make_async_copy(ref, x_buf.at[i], x_sem.at[i]) for i, ref in enumerate((own_ref, other_ref))]
    w_copies[0].start()
    x_copies[0].start()
    w_copies[0].wait()
    x_copies[1].start()
    w_copies[1].start()
    for z in range(N_Z):
        rows = slice(z * BLOCK, (z + 1) * BLOCK)
        w_high[rows], w_low[rows] = split(w_in_buf[z] * gain_ref[...])
    position = iota((LMAX, 1), 0)

    keeps, slope_bufs = (keep_even, keep_odd), (slope_even, slope_odd)

    def store_from(buf, parity, step):
        rows = slice(step * TOKENS, (step + 1) * TOKENS)
        return pltpu.make_async_copy(buf, slope_ref.at[rows], slope_sem.at[parity])

    def tokens_of(step):
        start = step % (STEPS // 2) * TOKENS
        return x_buf[step // (STEPS // 2), start : start + TOKENS]

    def product(step, keep):
        x = tokens_of(step)
        for j in range(HALF // 256):
            cols = slice(j * 256, (j + 1) * 256)
            keep[:, cols] = dot(x, w_high[cols], NT) + dot(x, w_low[cols], NT)

    def turn(step, now, later, slope_out, copy):
        if step >= 2:
            copy(step - 2).wait()
        if step + 1 < STEPS:
            product(step + 1, later)
        xf = tokens_of(step).astype(f32)
        inverse = lax.rsqrt(jnp.sum(xf * xf, axis=1, keepdims=True) * (1.0 / D) + 1e-05)
        weights = []
        for i in range(TEXTS_STEP):
            length = lengths_ref[step * TEXTS_STEP + i]
            scale = 1.0 / jnp.full((1, 1), length, jnp.int32).astype(f32)
            weights.append(jnp.where(position < length, scale, 0.0))
            rows = slice(i * LMAX, (i + 1) * LMAX)
            pooled_x[step, i : i + 1] = jnp.sum(xf[rows] * weights[i], axis=0, keepdims=True)
        weight = jnp.concatenate(weights, axis=0)
        scaled = weight * inverse
        for j in range(HALF // 256):
            cols = slice(j * 256, (j + 1) * 256)
            p = now[:, cols] * inverse
            p2 = p * p
            half = 0.5 + 0.5 * jnp.tanh(p * (C0 + C1 * p2))
            act = p * half
            slope = half + (act - act * half) * (2.0 * C0 + 6.0 * C1 * p2)
            slope_out[:, cols] = slope * scaled
            act = act * weight
            for i in range(TEXTS_STEP):
                rows = slice(i * LMAX, (i + 1) * LMAX)
                pooled[step, i : i + 1, cols] = jnp.sum(act[rows], axis=0, keepdims=True)
        copy(step).start()

    x_copies[0].wait()
    product(0, keeps[0])
    for step in range(STEPS):
        if step == STEPS // 2 - 1:
            x_copies[1].wait()
        parity = step % 2
        store = functools.partial(store_from, slope_bufs[parity], parity)
        turn(step, keeps[parity], keeps[1 - parity], slope_bufs[parity], store)
    w_copies[1].wait()
    acts = jnp.concatenate([pooled[i] for i in range(STEPS)], axis=0)
    total = 0.5 * jnp.concatenate([pooled_x[i] for i in range(STEPS)], axis=0)
    for z in range(N_Z):
        high, low = split(w_out_buf[z])
        out_high_ref[z] = high
        out_low_ref[z] = low
        a = acts[:, z * BLOCK : (z + 1) * BLOCK]
        pooled_ref[z] = jnp.concatenate([a, jnp.zeros((2 * TXT, 256 - BLOCK), f32)], axis=1)
        a_high, a_low = split(a)
        total = total + (dot(a_high, high, NN) + (dot(a_high, low, NN) + dot(a_low, high, NN)))
    sums_ref[...] = total
    for parity in range(2):
        store_from(slope_bufs[parity], parity, STEPS - 2 + parity).wait()


def forward(place, lengths, gain, own, other, w_in, w_out):
    tokens = 2 * TXT * LMAX
    shape = jax.ShapeDtypeStruct
    return pl.pallas_call(
        forward_kernel,
        out_shape=(
            pltpu.HBM((tokens, HALF), f32),
            shape((N_Z, 2 * TXT, 256), f32),
            shape((2 * TXT, D), f32),
            shape((N_Z, BLOCK, D), bf16),
            shape((N_Z, BLOCK, D), bf16),
        ),
        in_specs=smem(2) + vmem(1) + [HBM] * 4,
        out_specs=(HBM, *vmem(4)),
        scratch_shapes=[
            pltpu.VMEM((N_Z, BLOCK, D), f32),
            pltpu.VMEM((N_Z, BLOCK, D), f32),
            pltpu.VMEM((2, TXT * LMAX, D), bf16),
            pltpu.VMEM((TOKENS, HALF), f32),
            pltpu.VMEM((TOKENS, HALF), f32),
            pltpu.VMEM((TOKENS, HALF), f32),
            pltpu.VMEM((TOKENS, HALF), f32),
            pltpu.VMEM((HALF, D), bf16),
            pltpu.VMEM((HALF, D), bf16),
            pltpu.VMEM((STEPS, TEXTS_STEP, HALF), f32),
            pltpu.VMEM((STEPS, TEXTS_STEP, D), f32),
            pltpu.SemaphoreType.DMA((2,)),
            pltpu.SemaphoreType.DMA((2,)),
            pltpu.SemaphoreType.DMA((2,)),
        ],
        compiler_params=params(24),
        cost_estimate=cost(10 * tokens * HALF * D, 8 * 10**6),
        name="encoder_forward",
    )(place, lengths, gain, in_hbm(own), in_hbm(other), in_hbm(w_in), in_hbm(w_out))


def unit_rows(sums):
    return lax.rsqrt(jnp.sum(sums * sums, axis=-1, keepdims=True) + 1e-06)


def each_label(owners_ref, counts, put, first=0):
    for o in range(N_LABEL):
        counts[o] = 0
    for i in range(TXT):
        owner = owners_ref[first + i]
        rank = counts[owner]
        counts[owner] = rank + 1
        put(i, owner, jnp.minimum(rank, CAP - 1))


def label_kernel(owners_ref, part_ref, came_ref, free_ref, sums_ref, out_ref, counts):
    own = part_ref[:TXT] + came_ref[TXT:]
    sums_ref[:TXT] = own
    sums_ref[TXT:] = part_ref[TXT:] + came_ref[:TXT]
    scaled = (own * unit_rows(own) + free_ref[...]) * LABEL_SCALE
    out_ref[...] = jnp.zeros_like(out_ref)

    def put(i, owner, rank):
        first = owner // 8 * (8 * SLOT_ROWS) + rank * (8 * PIECES) + lax.rem(owner, 8)
        for j in range(PIECES):
            out_ref[pl.ds(first + 8 * j, 1)] = scaled[i : i + 1, j * 128 : (j + 1) * 128]

    each_label(owners_ref, counts, put)


def labels(owners, part, came, free_vectors):
    return pl.pallas_call(
        label_kernel,
        out_shape=(
            jax.ShapeDtypeStruct((2 * TXT, D), f32),
            jax.ShapeDtypeStruct((N_LABEL * SLOT_ROWS, 128), f32),
        ),
        in_specs=smem(1) + vmem(3),
        out_specs=tuple(vmem(2)),
        scratch_shapes=[pltpu.SMEM((N_LABEL,), jnp.int32)],
        compiler_params=params(8),
        cost_estimate=cost(10**6, 8 * 10**5),
        name="label_vectors",
    )(owners, part, came, free_vectors)


def scores_kernel(place_ref, shortlist_ref, queries_ref, own_ref, other_ref, out_ref):
    size = 2 * CHIP_SLOTS
    column = iota((size, size), 0)
    rank = column % CAP
    lab = column // CAP % N_LABEL
    core = column // (CAP * N_LABEL) % N_CORE
    z = column // (CAP * N_LABEL * N_CORE)
    half = jnp.where(core == place_ref[0], 0, 1)
    source = half * CHIP_SLOTS + rank * N_CHIPS + z * N_LABEL + lab
    order = (iota((size, size), 1) == source).astype(bf16)
    table = jnp.concatenate(
        [
            jnp.concatenate(
                [ref[pl.ds(PIECES * r + j, N_CHIPS, stride=SLOT_ROWS)] for j in range(PIECES)],
                axis=1,
            )
            for ref in (own_ref, other_ref)
            for r in range(CAP)
        ],
        axis=0,
    )
    t_high, t_low = (dot(order, part, NN).astype(bf16) for part in split(table))
    q_high, q_low = split(queries_ref[...])
    scores = dot(q_high, t_high, NT) + (dot(q_high, t_low, NT) + dot(q_low, t_high, NT))
    out_ref[...] = scores * is_kept(shortlist_ref, place_ref[1])


def slot_scores(place, shortlist, queries, own, other):
    return pl.pallas_call(
        scores_kernel,
        out_shape=jax.ShapeDtypeStruct((QROWS, 2 * CHIP_SLOTS), f32),
        in_specs=smem(1) + vmem(4),
        out_specs=pl.BlockSpec(memory_space=pltpu.VMEM),
        compiler_params=params(24),
        cost_estimate=cost(6 * QROWS * 256 * D, 4 * 10**6),
        name="slot_scores",
    )(place, shortlist, queries, own, other)


def return_kernel(place_ref, owners_ref, came_ref, out_ref, counts):
    for h in range(N_CORE):
        core = place_ref[0] if h == 0 else 1 - place_ref[0]

        def put(i, owner, rank, h=h, core=core):
            value = came_ref[owner]
            for z in range(1, N_Z):
                value = value + came_ref[z * N_LABEL + owner]
            value = jnp.where(core == 0, value[:SLOT_ROWS], value[SLOT_ROWS:])
            value = jnp.where(rank == 0, value[:PIECES], value[PIECES:])
            row = h * TXT + i
            for j in range(PIECES):
                out_ref[row : row + 1, j * 128 : (j + 1) * 128] = value[j : j + 1]

        each_label(owners_ref, counts, put, h * TXT)


def returned(place, owners, came):
    return pl.pallas_call(
        return_kernel,
        out_shape=jax.ShapeDtypeStruct((2 * TXT, D), f32),
        in_specs=smem(2) + vmem(1),
        out_specs=pl.BlockSpec(memory_space=pltpu.VMEM),
        scratch_shapes=[pltpu.SMEM((N_LABEL,), jnp.int32)],
        compiler_params=params(8),
        cost_estimate=cost(10**5, 5 * 10**5),
        name="returned_gradients",
    )(place, owners, came)


def pull_kernel(place_ref, free_ref, came_ref, sums_ref, pooled_ref, labels_ref, pulled_ref, joined_ref, *outs):
    own = free_ref[:TXT] + came_ref[TXT:]
    joined_ref[...] = own
    free = jnp.concatenate([own, free_ref[TXT:] + came_ref[:TXT]], axis=0)
    sums = sums_ref[...]
    unit = unit_rows(sums)
    along = jnp.sum(sums * free, axis=-1, keepdims=True)
    pulled = unit * free - (unit * unit * unit * along) * sums
    pulled_ref[...] = pulled
    for f in range(N_Z):
        acts = pooled_ref[lax.rem(place_ref[4] + f, N_Z)]
        for k in range(FACTOR_ROWS // (2 * TXT)):
            piece = acts[:, k * 128 : (k + 1) * 128] if k < 2 else pulled[:, (k - 2) * 128 : (k - 1) * 128]
            outs[f][k * 2 * TXT : (k + 1) * 2 * TXT] = piece
        outs[f][FACTOR_ROWS:] = labels_ref[...]


def pull(place, free, came, sums, pooled, label_rows):
    return pl.pallas_call(
        pull_kernel,
        out_shape=(jax.ShapeDtypeStruct((2 * TXT, D), f32), jax.ShapeDtypeStruct((TXT, D), f32))
        + (jax.ShapeDtypeStruct((MOVED_ROWS, 128), f32),) * N_Z,
        in_specs=smem(1) + vmem(5),
        out_specs=tuple(vmem(2 + N_Z)),
        compiler_params=params(12),
        cost_estimate=cost(6 * 32 * HALF * D, 3 * 10**6),
        name="pull_back",
    )(place, free, came, sums, pooled, label_rows)


def w_out_kernel(pulled_ref, joined_ref, high_ref, low_ref, back_ref, free_grad_ref):
    free_grad_ref[...] = joined_ref[...]
    p_high, p_low = split(pulled_ref[...])
    back_ref[...] = jnp.concatenate(
        [
            dot(p_high, high_ref[z], NT) + (dot(p_high, low_ref[z], NT) + dot(p_low, high_ref[z], NT))
            for z in range(N_Z)
        ],
        axis=1,
    )


def through_w_out(pulled, joined, high, low):
    return pl.pallas_call(
        w_out_kernel,
        out_shape=(jax.ShapeDtypeStruct((2 * TXT, HALF), f32), jax.ShapeDtypeStruct((TXT, D), f32)),
        in_specs=vmem(4),
        out_specs=tuple(vmem(2)),
        compiler_params=params(12),
        cost_estimate=cost(6 * 32 * HALF * D, 3 * 10**6),
        name="back_through_w_out",
    )(pulled, joined, high, low)


def backward_kernel(back_ref, gain_ref, own_ref, other_ref, slope_ref, grad, largest, x_buf, slope_buf, sem):
    copies = []
    for q in range(PARTS):
        x_rows = slice(q % (PARTS // 2) * PART, (q % (PARTS // 2) + 1) * PART)
        x_ref = (own_ref, other_ref)[q // (PARTS // 2)]
        rows = slice(q * PART, (q + 1) * PART)
        copies.append(
            (
                pltpu.make_async_copy(x_ref.at[x_rows], x_buf.at[q], sem.at[0, q]),
                pltpu.make_async_copy(slope_ref.at[rows], slope_buf.at[q], sem.at[1, q]),
            )
        )
    for copy in copies[0]:
        copy.start()
    for q in range(PARTS):
        for copy in copies[q]:
            copy.wait()
        if q + 1 < PARTS:
            for copy in copies[q + 1]:
                copy.start()

        def product(j):
            cols = slice(j * 256, (j + 1) * 256)
            total = jnp.zeros((256, D), f32)
            for i in range(PART // TOKENS):
                pieces = []
                for t in range(i * TEXTS_STEP, (i + 1) * TEXTS_STEP):
                    text = q * (PART // LMAX) + t
                    pieces.append(slope_buf[q, t * LMAX : (t + 1) * LMAX, cols] * back_ref[text : text + 1, cols])
                high, low = split(jnp.concatenate(pieces, axis=0))
                x = x_buf[q, i * TOKENS : (i + 1) * TOKENS]
                total = total + (dot(high, x, TN) + dot(low, x, TN))
            if q > 0:
                total = total + grad[cols]
            if q == PARTS - 1:
                total = total * gain_ref[...]
                largest[j : j + 1] = jnp.max(jnp.abs(total), axis=0, keepdims=True)
            grad[cols] = total

        for j in range(HALF // 256):
            product(j)


def backward(back, gain, own, other, slope):
    tokens = 2 * TXT * LMAX
    shape = jax.ShapeDtypeStruct
    return pl.pallas_call(
        backward_kernel,
        out_shape=(shape((HALF, D), f32), shape((HALF // 256, D), f32)),
        in_specs=vmem(2) + [HBM] * 3,
        out_specs=tuple(vmem(2)),
        scratch_shapes=[
            pltpu.VMEM((PARTS, PART, D), bf16),
            pltpu.VMEM((PARTS, PART, HALF), f32),
            pltpu.SemaphoreType.DMA((2, PARTS)),
        ],
        compiler_params=params(24),
        cost_estimate=cost(5 * tokens * HALF * D, 4 * 10**6),
        name="encoder_backward",
    )(back, gain, in_hbm(own), in_hbm(other), in_hbm(slope))


def power_of(top):
    return jnp.clip(jnp.floor(14.0 - jnp.log2(jnp.maximum(top, 1e-30))), -100.0, 100.0)


def finish_kernel(grad_ref, largest_ref, *rest):
    factors, out_ref = rest[:N_Z], rest[N_Z]
    wide = jnp.concatenate(
        [
            jnp.concatenate([ref[k * 2 * TXT : (k + 1) * 2 * TXT] for ref in factors], axis=0)
            for k in range(FACTOR_ROWS // (2 * TXT))
        ],
        axis=1,
    )
    block = dot3(wide[:, :BLOCK], wide[:, 256:], TN)
    top = jnp.max(jnp.max(largest_ref[...], axis=0, keepdims=True), axis=1, keepdims=True)
    block_top = jnp.max(jnp.max(jnp.abs(block), axis=0, keepdims=True), axis=1, keepdims=True)
    power, block_power = power_of(top), power_of(block_top)
    scale = jnp.exp2(power)
    block = block * jnp.exp2(block_power)
    powers = jnp.where(iota((8, 128), 0) < 4, power, block_power)
    for lab in range(N_LABEL):
        first = lab * SENT_ROWS
        for j in range(PIECES):
            start = first + AT_W_OUT + j * ROWS
            out_ref[start : start + ROWS] = block[lab * ROWS : (lab + 1) * ROWS, j * 128 : (j + 1) * 128]
        out_ref[first + AT_POWERS : first + AT_LABELS] = powers
    for f in range(N_Z):
        for g in range(N_LABEL // 8):
            for k in range(SLOT_ROWS):
                start = g * 8 * SENT_ROWS + AT_LABELS + f * SLOT_ROWS + k
                row = FACTOR_ROWS + (g * SLOT_ROWS + k) * 8
                out_ref[pl.ds(start, 8, stride=SENT_ROWS)] = factors[f][row : row + 8]
    for z in range(N_Z):
        for k in range(N_LABEL // 2):
            start = z * BLOCK + k * 2 * ROWS
            rows = grad_ref[start : start + 2 * ROWS] * scale
            for g in range(2):
                for j in range(PIECES):
                    piece = rows[g * ROWS : (g + 1) * ROWS, j * 128 : (j + 1) * 128]
                    first = (2 * k + g) * SENT_ROWS + z * CHUNK + j * ROWS
                    out_ref[first : first + ROWS] = piece


def finish(grad, largest, factors):
    return pl.pallas_call(
        finish_kernel,
        out_shape=jax.ShapeDtypeStruct((N_LABEL * SENT_ROWS, 128), f32),
        in_specs=vmem(2 + N_Z),
        out_specs=pl.BlockSpec(memory_space=pltpu.VMEM),
        compiler_params=params(16),
        cost_estimate=cost(10**9, 5 * 10**6),
        name="finish_gradients",
    )(grad, largest, *factors)


def unpieced(rows):
    return jnp.concatenate([rows[j * ROWS : (j + 1) * ROWS] for j in range(PIECES)], axis=1)


def middle_kernel(place_ref, came_ref, w_out_ref, table_ref, *outs):
    total = jnp.zeros((AT_W_OUT, 128), f32)
    block = jnp.zeros((CHUNK, 128), f32)
    for lab in range(N_LABEL):
        total = total + came_ref[lab, :AT_W_OUT] * jnp.exp2(-came_ref[lab, AT_POWERS : AT_POWERS + 1])
        block = block + came_ref[lab, AT_W_OUT:AT_POWERS] * jnp.exp2(-came_ref[lab, AT_POWERS + 4 : AT_POWERS + 5])
    w_out_ref[...] = unpieced(block)
    for f in range(N_Z):
        z = lax.rem(place_ref[4] - f + N_Z, N_Z)
        for lab in range(N_LABEL):
            first = AT_LABELS + f * SLOT_ROWS
            table_ref[z, lab * SLOT_ROWS : (lab + 1) * SLOT_ROWS] = came_ref[lab, first : first + SLOT_ROWS] * (
                1.0 / LABEL_SCALE
            )
    for z in range(N_Z):
        for f in range(N_Z):

            @pl.when(lax.rem(place_ref[4] + f, N_Z) == z)
            def _(z=z, f=f):
                outs[f][...] = total[z * CHUNK : (z + 1) * CHUNK]


def middle(place, came):
    return pl.pallas_call(
        middle_kernel,
        out_shape=(
            jax.ShapeDtypeStruct((ROWS, D), f32),
            jax.ShapeDtypeStruct((N_Z, N_LABEL * SLOT_ROWS, 128), f32),
        )
        + (jax.ShapeDtypeStruct((CHUNK, 128), f32),) * N_Z,
        in_specs=smem(1) + vmem(1),
        out_specs=tuple(vmem(2 + N_Z)),
        compiler_params=params(16),
        cost_estimate=cost(10**7, 4 * 10**6),
        name="plane_sums",
    )(place, came)


def last_kernel(*rest):
    blocks, w_in_ref = rest[:N_Z], rest[-1]
    w_in_ref[...] = unpieced((blocks[0][...] + blocks[1][...]) + (blocks[2][...] + blocks[3][...]))


def last(blocks, after):
    return pl.pallas_call(
        last_kernel,
        out_shape=jax.ShapeDtypeStruct((ROWS, D), f32),
        in_specs=vmem(N_Z) + [HBM],
        out_specs=pl.BlockSpec(memory_space=pltpu.VMEM),
        compiler_params=params(8),
        cost_estimate=cost(10**6, 10**6),
        name="z_sums",
    )(*blocks, in_hbm(after))


def swap(value):
    return lax.ppermute(value, "core", ((0, 1), (1, 0)))


def shift(blocks, axis):
    moved = [lax.ppermute(blocks[k], axis, [(i, (i + k) % 4) for i in range(4)]) for k in range(1, 4)]
    return [blocks[0]] + moved


def exchange(value, axes):
    return lax.all_to_all(value, axes, split_axis=0, concat_axis=0, tiled=True)


def local(texts, lengths, owners, gain, w_in, w_out, free_vectors, queries, shortlist, grad_scores):
    core, x, y, z = (lax.axis_index(name) for name in ("core", "x", "y", "z"))
    place = jnp.stack([core, x * N_Y + y, x, y, z]).astype(jnp.int32)
    own = texts.reshape(TXT * LMAX, D)
    other = swap(own)
    ints = jnp.stack([lengths, owners[:, 0]])
    ints_other = swap(ints)
    both_lengths = jnp.concatenate([ints[0], ints_other[0]])
    owner_ids = jnp.concatenate([ints[1], ints_other[1]])
    names = shortlist.T
    gain_row = gain.reshape(1, D)
    w_in_blocks = w_in.reshape(N_Z, N_CORE, BLOCK, D)
    w_out_blocks = w_out.reshape(N_Z, N_CORE, BLOCK, D)

    slots = slot_partials(place, names, grad_scores, queries).reshape(N_CHIPS, CHIP_ROWS, 128)
    slots = exchange(slots, ("z", "x", "y"))

    slope, pooled, part, high, low = forward(place, both_lengths, gain_row, own, other, w_in_blocks, w_out_blocks)
    sums, label_rows = labels(owner_ids, part, swap(part), free_vectors)

    free = returned(place, owner_ids, slots)
    pulled, joined, *factors = pull(place, free, swap(free), sums, pooled, label_rows)
    back, free_grad = through_w_out(pulled, joined, high, low)
    factors = shift(factors, "z")
    grad, largest = backward(back, gain_row, own, other, slope)
    sent_rows = finish(grad, largest, factors).reshape(N_LABEL, SENT_ROWS, 128)
    came = exchange(sent_rows.astype(jnp.float16), LABEL).astype(f32)
    w_out_grad, table, *moved = middle(place, came)
    table = table.reshape(N_CHIPS * SLOT_ROWS, 128)
    moved = shift(moved, "z")
    scores = slot_scores(place, names, queries, table, swap(table))
    w_in_grad = last(moved, scores)
    return scores, free_grad, w_in_grad, w_out_grad


def solution(mesh):
    fine = Mesh(mesh.devices.reshape(N_Z, N_CORE, N_X, N_Y), ("z", "core", "x", "y"))
    dp, every = ("z", "core"), ("z", "core", "x", "y")
    placed = (
        P(every, None, None),
        P(every),
        P(every, None),
        P(),
        P(),
        P(),
        P(every, None),
        P(dp, None),
        P(dp, None),
        P(dp, LABEL),
    )
    return jax.shard_map(
        local,
        mesh=fine,
        in_specs=placed,
        out_specs=(
            P(dp, LABEL),
            P(every, None),
            P(every, None),
            P(every, None),
        ),
        check_vma=False,
    )
```
